256 devices in a mesh: dp: 64 (over z_lo, y, x, core), grp: 4 (over z_hi).
Axes of the slice: x: 4, y: 4, z: 8 (z_hi: 4, z_lo: 2; z = z_hi * 2 + z_lo), core: 2. Of those that a mesh axis runs over, the one named last changes fastest.
Arguments:
- patches: bfloat16 [1, 524288, 1152], P(None, ('dp', 'grp')), may hold values from -24 to 24
- out_grads: bfloat16 [1, 524288, 128], P(None, ('dp', 'grp')), may hold values from -6 to 6
- counts: int32 [256], P(('dp', 'grp')), may hold values from 682 to 2048, as said below
- basis_a: bfloat16 [1, 1152, 1152], replicated, may hold values from -0.1875 to 0.1875
- basis_g: bfloat16 [1, 128, 128], replicated, may hold values from -0.5 to 0.5
- eig_a: float32 [1, 1152], replicated, may hold values from 0.5 to 5
- eig_g: float32 [1, 128], replicated, may hold values from 0.001 to 0.01
Outputs:
- a_factor: float32 [1, 1152, 1152], P(None, 'dp')
- g_factor: float32 [1, 128, 128], replicated
- precond: float32 [1, 128, 1152], replicated
The draws below stay inside these ranges and needn't reach their ends.
Inputs may be any that keep to these rules, and one draw needn't show every extreme that they name: counts rise roughly evenly with the device index from about 2048 // 3 to 2048; the last device has exactly 2048.
All inputs are finite; a program needn't handle non-finite values.
Results may differ from the reference program's by a relative error of at most 0.0065.
Values sent between devices are 32-bit elements; how exact they have to be, the bound alone decides.
No kernel may reach another device: no remote copies, remote signals or barrier semaphores. Data moves between devices by JAX's collectives and lax.ppermute only.
A program may use at most 64 MiB of HBM per device.

```python
import math
import jax
import jax.numpy as jnp
from jax import lax

DA = 1152
DG = 128
LAYERS = 1
ROWS = 2048
TOKENS = 524288
DEVICES = 256


def draw_counts(key, part):
    key = jax.random.fold_in(key, 7)
    lowest = ROWS // 3
    index = jnp.arange(DEVICES, dtype=jnp.int32)
    rising = lowest + index * (ROWS - lowest) // max(DEVICES - 1, 1)
    jitter = jax.random.randint(key, (DEVICES,), 0, max(ROWS // 4, 2), dtype=jnp.int32)
    values = jnp.maximum(rising - jitter, lowest)
    return jnp.where(index == DEVICES - 1, ROWS, values).astype(jnp.int32)


def with_spikes(values, own_key, source, target, parts, factor):
    owner, partner = [(jnp.arange(values.shape[dim]) // (values.shape[dim] // parts)).reshape([-1 if axis == dim else 1 for axis in range(values.ndim)]) for dim in (source, target)]
    chosen = jax.random.permutation(own_key, parts)[partner]
    strong = (owner == chosen) | (owner == (partner + parts // 2) % parts)
    return jnp.where(strong, factor * values, values)


def shard_levels(own_key, dims, split, low, largest):
    factor_of, own = 1.0, jax.random.fold_in(own_key, 6)
    for axis_at, shards_of in split:
        steps = jnp.exp(jax.random.uniform(jax.random.fold_in(own, axis_at), (shards_of,), jnp.float32, low / len(split), largest / len(split)))
        factor_of = factor_of * jnp.repeat(steps, dims[axis_at] // shards_of).reshape([-1 if axis == axis_at else 1 for axis in range(len(dims))])
    return factor_of


def gaussian(own_key, dims, width, most, split=(), kind=jnp.bfloat16):
    values = jax.random.normal(own_key, dims, jnp.float32) * width
    if len(split) > 0:
        values = shard_levels(own_key, dims, split, -0.22, 0.18) * values
    return jnp.clip(values, min=-most, max=most).astype(kind)


def heavy_noise(rng, dims, spread, reach, cuts, heavy, kind=jnp.bfloat16):
    result = spread * jax.random.normal(rng, dims, jnp.float32)
    if cuts:
        result = result * shard_levels(rng, dims, cuts, -0.22, 0.18)
    return jnp.clip(with_spikes(result, jax.random.fold_in(rng, 3), *heavy), -reach, reach).astype(kind)


def setup_inputs(seed: int = 0) -> dict:
    key_of = jax.random.split(jax.random.key(seed), 8)
    patches = heavy_noise(key_of[0], (LAYERS, TOKENS, DA), 1.0, 24.0, ((1, 256),), (1, 2, 128, 5.5))
    out_grads = gaussian(key_of[1], (LAYERS, TOKENS, DG), 1.0, 6.0, ((1, 256),))
    counts = draw_counts(jax.random.fold_in(key_of[7], 71), 0)
    basis_a = gaussian(key_of[3], (LAYERS, DA, DA), DA ** -0.5, 0.1875)
    basis_g = gaussian(key_of[4], (LAYERS, DG, DG), DG ** -0.5, 0.5)
    eig_a = jnp.clip(jnp.exp(jax.random.uniform(key_of[5], (LAYERS, DA), jnp.float32, math.log(0.5), math.log(5.0))), 0.5, 5.0)
    eig_g = jnp.clip(jnp.exp(jax.random.uniform(key_of[6], (LAYERS, DG), jnp.float32, math.log(0.001), math.log(0.01))), 0.001, 0.01)
    return {"patches": patches, "out_grads": out_grads, "counts": counts, "basis_a": basis_a, "basis_g": basis_g, "eig_a": eig_a, "eig_g": eig_g}


def reference(patches, out_grads, counts, basis_a, basis_g, eig_a, eig_g):
    devices_all = counts.shape[0]
    rows = patches.shape[1] // devices_all
    valid = (jnp.arange(rows, dtype=jnp.int32)[None, :] < counts[:, None]).reshape(-1)[:, None]
    total = jnp.sum(counts.astype(jnp.float32))
    a_list, g_list, p_list = [], [], []
    for layer in range(patches.shape[0]):
        masked_x = jnp.where(valid, patches[layer], jnp.zeros((), jnp.bfloat16))
        masked_y = jnp.where(valid, out_grads[layer], jnp.zeros((), jnp.bfloat16))
        contract = (((0,), (0,)), ((), ()))
        a_list.append(lax.dot_general(masked_x, masked_x, contract, preferred_element_type=jnp.float32) / total)
        g_list.append(lax.dot_general(masked_y, masked_y, contract, preferred_element_type=jnp.float32) / total)
        grad = (lax.dot_general(masked_y, masked_x, contract, preferred_element_type=jnp.float32) / total).astype(jnp.bfloat16)
        left = lax.dot_general(basis_g[layer], grad, contract, preferred_element_type=jnp.float32).astype(jnp.bfloat16)
        rotated = jnp.dot(left, basis_a[layer], preferred_element_type=jnp.float32)
        scaled = (rotated / (eig_g[layer][:, None] * eig_a[layer][None, :] + 0.001)).astype(jnp.bfloat16)
        inner = jnp.dot(basis_g[layer], scaled, preferred_element_type=jnp.float32).astype(jnp.bfloat16)
        p_list.append(lax.dot_general(inner, basis_a[layer], (((1,), (1,)), ((), ())), preferred_element_type=jnp.float32))
    return jnp.stack(a_list), jnp.stack(g_list), jnp.stack(p_list)
```

```python
import functools

import jax
import jax.numpy as jnp
from jax import lax
from jax.experimental import pallas as pl
from jax.experimental.pallas import tpu as pltpu
from jax.sharding import Mesh, PartitionSpec as P

DA, DG, ROWS = 1152, 128, 2048
WIDTH = DA + DG
CHIPS, SLOTS, GRADS = 32, 24, 3
CHIP_AXES = ("zl", "y", "xh", "xl")
HBM = pltpu.MemorySpace.HBM
F32, BF16 = jnp.float32, jnp.bfloat16


def factor_place(row8, col):
    group, within = row8 // 9, (row8 % 9) * 9 + col
    if within < 20:
        return 0, 2 * group, GRADS + within
    if within < 40:
        return 0, 2 * group + 1, GRADS + within - 20
    if within < 61:
        return 1, 2 * group, GRADS + within - 40
    return 1, 2 * group + 1, GRADS + within - 61


def grad_place(row8, col):
    chip, rest = divmod(row8 * 10 + col, 5)
    return (0, chip, rest) if rest < 3 else (1, chip, rest - 3)


def gram_kernel(parts, block, count_ref, core_ref, x_hbm, y_hbm, mine, theirs, z, zt, acc, in_sem, out_sem):
    step = ROWS // parts
    copies = []
    for k in range(parts):
        rows = pl.ds(k * step, step)
        copies.append(
            (
                pltpu.make_async_copy(x_hbm.at[0, rows, :], z.at[rows, pl.ds(0, DA)], in_sem.at[k, 0]),
                pltpu.make_async_copy(y_hbm.at[0, rows, :], z.at[rows, pl.ds(DA, DG)], in_sem.at[k, 1]),
            )
        )
        for copy in copies[k]:
            copy.start()
    count, core = count_ref[0], core_ref[0]
    for k in range(parts):
        for copy in copies[k]:
            copy.wait()
        here = slice(k * step, (k + 1) * step)
        row = lax.broadcasted_iota(jnp.int32, (step, 1), 0) + k * step
        zt[:, here] = jnp.where(row < count, z[here, :], jnp.zeros((), BF16)).T
    acc[0, :, SLOTS - 1, :, :] = jnp.full((CHIPS, 8, 128), count.astype(F32))
    acc[1, :, SLOTS - 1, :, :] = jnp.zeros((CHIPS, 8, 128), F32)
    acc[1, :, GRADS - 1, :, :] = jnp.full((CHIPS, 8, 128), count.astype(F32))
    for i in range(0, WIDTH, block):
        for j in range(0, WIDTH, block):
            if i + block <= DA and j >= DA:
                continue
            w = jnp.dot(zt[i : i + block, :], z[:, j : j + block], preferred_element_type=F32)
            for u in range(block // 8):
                row8 = i // 8 + u
                for v in range(block // 128):
                    col = j // 128 + v
                    tile = w[8 * u : 8 * u + 8, 128 * v : 128 * v + 128]
                    if row8 >= DA // 8:
                        acc[grad_place(row8 - DA // 8, col)] = tile
                    elif col < DA // 128:
                        acc[factor_place(row8, col)] = tile
    first = pltpu.make_async_copy(acc.at[1 - core], theirs, out_sem.at[0])
    second = pltpu.make_async_copy(acc.at[core], mine, out_sem.at[1])
    first.start()
    second.start()
    first.wait()
    second.wait()


def gram(patches, out_grads, counts, core):
    parts = 4
    half = jax.ShapeDtypeStruct((CHIPS, SLOTS, 8, 128), F32)
    return pl.pallas_call(
        functools.partial(gram_kernel, parts, 256),
        out_shape=(half, half),
        in_specs=[pl.BlockSpec(memory_space=pltpu.SMEM)] * 2 + [pl.BlockSpec(memory_space=HBM)] * 2,
        out_specs=(pl.BlockSpec(memory_space=HBM),) * 2,
        scratch_shapes=[
            pltpu.VMEM((ROWS, WIDTH), BF16),
            pltpu.VMEM((WIDTH, ROWS), BF16),
            pltpu.VMEM((2, CHIPS, SLOTS, 8, 128), F32),
            pltpu.SemaphoreType.DMA((parts, 2)),
            pltpu.SemaphoreType.DMA((2,)),
        ],
        compiler_params=pltpu.CompilerParams(vmem_limit_bytes=40 * 2**20),
        cost_estimate=pl.CostEstimate(flops=2 * ROWS * WIDTH * WIDTH, bytes_accessed=12 * 2**20, transcendentals=0),
        name="gram",
    )(counts, core, patches, out_grads)


def precond_kernel(g0, g1, total_ref, basis_a, basis_g, eig_a, eig_g, g_factor, precond):
    total = total_ref[:, :]
    halves = (g0[...].reshape(16, 2, GRADS, 8, 128), g1[...].reshape(16, 2, GRADS, 8, 128))
    columns = []
    for col in range(WIDTH // 128):
        n, rest = divmod(col, 5)
        tiles = halves[0][:, n, rest] if rest < 3 else halves[1][:, n, rest - 3]
        columns.append(tiles.reshape(128, 128) / total)
    g_factor[0] = columns[-1]
    grad = jnp.concatenate([c.astype(BF16) for c in columns[:-1]], axis=1)
    left = lax.dot_general(basis_g[0], grad, (((0,), (0,)), ((), ())), preferred_element_type=F32).astype(BF16)
    rotated = jnp.dot(left, basis_a[0], preferred_element_type=F32)
    scaled = (rotated / (eig_g[...] * eig_a[...] + 0.001)).astype(BF16)
    inner = jnp.dot(basis_g[0], scaled, preferred_element_type=F32).astype(BF16)
    precond[0] = lax.dot_general(inner, basis_a[0], (((1,), (1,)), ((), ())), preferred_element_type=F32)


def precondition(g0, g1, total, basis_a, basis_g, eig_a, eig_g):
    return pl.pallas_call(
        precond_kernel,
        out_shape=(jax.ShapeDtypeStruct((1, DG, DG), F32), jax.ShapeDtypeStruct((1, DG, DA), F32)),
        compiler_params=pltpu.CompilerParams(vmem_limit_bytes=40 * 2**20),
        name="precondition",
    )(g0, g1, total, basis_a, basis_g, eig_a, eig_g.reshape(DG, 1))


def rows_kernel(place_ref, own, by_core, by_x, by_both, total_ref, out, rows):
    place = place_ref[0]
    total = total_ref[...]
    got = (own, by_core, by_x, by_both)
    for here in range(4):
        xl, core = divmod(here, 2)

        @pl.when(place == here)
        def _():
            for row8 in range(9):
                for col in range(9):
                    c, n, slot = factor_place(row8, col)
                    tile = got[2 * (n ^ xl) + (c ^ core)][slot - GRADS]
                    rows[8 * row8 : 8 * row8 + 8, 128 * col : 128 * col + 128] = tile
            first = 36 * xl + 18 * core
            out[0] = rows[first : first + 18, :] / total[0:1, 0:1]


def factor_rows(place, own, by_core, by_x, by_both, total):
    vmem = pl.BlockSpec(memory_space=pltpu.VMEM)
    return pl.pallas_call(
        rows_kernel,
        out_shape=jax.ShapeDtypeStruct((1, 18, DA), F32),
        in_specs=[pl.BlockSpec(memory_space=pltpu.SMEM)] + [vmem] * 5,
        scratch_shapes=[pltpu.VMEM((72, DA), F32)],
        name="factor_rows",
    )(place, own, by_core, by_x, by_both, total)


def swap(value, axes):
    size = 2 ** len(axes)
    return lax.ppermute(value, axes, [(i, size - 1 - i) for i in range(size)])


def on_device(patches, out_grads, counts, basis_a, basis_g, eig_a, eig_g):
    core = lax.axis_index("core")
    xl = lax.axis_index("xl")
    mine, theirs = gram(patches, out_grads, counts, core[None])
    chip = mine + swap(theirs, ("core",))
    met = lax.all_to_all(chip, CHIP_AXES, 0, 0, tiled=True)
    part = jnp.sum(met, axis=0)
    copies = jnp.broadcast_to(part[None], (4, SLOTS, 8, 128))
    done = jnp.sum(lax.all_to_all(copies, "zh", 0, 0, tiled=True), axis=0)
    total = jnp.where(core == 0, done[SLOTS - 1, :1, :], done[GRADS - 1, :1, :])
    own = done[GRADS:]
    by_core = swap(own, ("core",))
    by_x = swap(own, ("xl",))
    by_both = swap(own, ("xl", "core"))
    sent = jnp.broadcast_to(done[None, :GRADS], (CHIPS, GRADS, 8, 128))
    grads = lax.all_to_all(sent, CHIP_AXES, 0, 0, tiled=True)
    other = swap(grads, ("core",))
    g0 = jnp.where(core == 0, grads, other)
    g1 = jnp.where(core == 0, other, grads)
    a_factor = factor_rows((2 * xl + core)[None], own, by_core, by_x, by_both, total)
    g_factor, precond = precondition(g0, g1, total, basis_a, basis_g, eig_a, eig_g)
    return a_factor, g_factor, precond


def solution(mesh):
    axes = ("zl", "y", "xh", "xl", "core", "zh")
    finer = Mesh(mesh.devices.reshape(2, 4, 2, 2, 2, 4), axes)
    placed = (P(None, axes, None), P(None, axes, None), P(axes), P(), P(), P(), P())
    return jax.shard_map(
        on_device,
        mesh=finer,
        in_specs=placed,
        out_specs=(P(None, axes[:-1], None), P(), P()),
        check_vma=False,
    )
```

```python
import functools

import jax
import jax.numpy as jnp
from jax import lax
from jax.experimental import pallas as pl
from jax.experimental.pallas import tpu as pltpu
from jax.sharding import Mesh, PartitionSpec as P

DA, DG, ROWS = 1152, 128, 2048
WIDTH = DA + DG
BLOCKS = DA // 128
HALF = BLOCKS // 2 + 1
CHIPS, SLOTS, GRADS = 32, 16, 3
HELD = 5
CHIP_AXES = ("zl", "y", "xh", "xl")
HBM = pltpu.MemorySpace.HBM
F32, BF16 = jnp.float32, jnp.bfloat16


def factor_places(row8, step):
    group, within = divmod(row8, 9)
    for xl in (0, 1):
        v = (within - 4 * xl) * HALF + step
        if 0 <= within - 4 * xl < HELD:
            yield (0, 2 * group + xl, GRADS + v) if v < 13 else (1, 2 * group + xl, GRADS + v - 13)


def grad_place(row8, col):
    chip, rest = divmod(row8 * 10 + col, 5)
    return (0, chip, rest) if rest < 3 else (1, chip, rest - 3)


def gram_kernel(parts, count_ref, place_ref, x_hbm, y_hbm, mine, theirs, z, zt, acc, in_sem, out_sem):
    step = ROWS // parts
    copies = []
    for k in range(parts):
        rows = pl.ds(k * step, step)
        copies.append(
            (
                pltpu.make_async_copy(x_hbm.at[0, rows, :], z.at[rows, pl.ds(0, DA)], in_sem.at[k, 0]),
                pltpu.make_async_copy(y_hbm.at[0, rows, :], z.at[rows, pl.ds(DA, DG)], in_sem.at[k, 1]),
            )
        )
        for copy in copies[k]:
            copy.start()
    count, core = count_ref[0], place_ref[2]
    for k in range(parts):
        for copy in copies[k]:
            copy.wait()
        here = slice(k * step, (k + 1) * step)
        row = lax.broadcasted_iota(jnp.int32, (step, 1), 0) + k * step
        zt[:, here] = jnp.where(row < count, z[here, :], jnp.zeros((), BF16)).T
    acc[1, :, SLOTS - 1, :, :] = jnp.zeros((CHIPS, 8, 128), F32)
    acc[1, :, GRADS - 1, :, :] = jnp.full((CHIPS, 8, 128), count.astype(F32))
    for col0 in range(0, BLOCKS + 1, 2):
        wanted = sorted({(c - s) % BLOCKS for c in (col0, col0 + 1) if c < BLOCKS for s in range(HALF)}) + [BLOCKS]
        runs = []
        for i in wanted:
            if runs and runs[-1][-1] == i - 1:
                runs[-1].append(i)
            else:
                runs.append([i])
        for run in runs:
            w = jnp.dot(
                zt[128 * run[0] : 128 * run[-1] + 128, :],
                z[:, 128 * col0 : 128 * col0 + 256],
                preferred_element_type=F32,
            )
            for u in range(16 * len(run)):
                row8 = 16 * run[0] + u
                for v in (0, 1):
                    tile = w[8 * u : 8 * u + 8, 128 * v : 128 * v + 128]
                    if row8 >= DA // 8:
                        acc[grad_place(row8 - DA // 8, col0 + v)] = tile
                    elif col0 + v < BLOCKS and (col0 + v - row8 // 16) % BLOCKS < HALF:
                        for place in factor_places(row8, (col0 + v - row8 // 16) % BLOCKS):
                            acc[place] = tile
    first = pltpu.make_async_copy(acc.at[1 - core], theirs, out_sem.at[0])
    second = pltpu.make_async_copy(acc.at[core], mine, out_sem.at[1])
    first.start()
    second.start()
    first.wait()
    second.wait()


def gram(patches, out_grads, counts, place):
    parts = 4
    half = jax.ShapeDtypeStruct((CHIPS, SLOTS, 8, 128), F32)
    return pl.pallas_call(
        functools.partial(gram_kernel, parts),
        out_shape=(half, half),
        in_specs=[pl.BlockSpec(memory_space=pltpu.SMEM)] * 2 + [pl.BlockSpec(memory_space=HBM)] * 2,
        out_specs=(pl.BlockSpec(memory_space=HBM),) * 2,
        scratch_shapes=[
            pltpu.VMEM((ROWS, WIDTH), BF16),
            pltpu.VMEM((WIDTH, ROWS), BF16),
            pltpu.VMEM((2, CHIPS, SLOTS, 8, 128), F32),
            pltpu.SemaphoreType.DMA((parts, 2)),
            pltpu.SemaphoreType.DMA((2,)),
        ],
        compiler_params=pltpu.CompilerParams(vmem_limit_bytes=60 * 2**20),
        cost_estimate=pl.CostEstimate(flops=2 * ROWS * WIDTH * WIDTH, bytes_accessed=10 * 2**20, transcendentals=0),
        name="gram",
    )(counts, place, patches, out_grads)


def spread_kernel(place_ref, done, twin, send, direct, total, flat):
    group, xl, core = place_ref[0], place_ref[1], place_ref[2]
    own, other = done[...], twin[...]
    low = jnp.where(core == 0, own, other)
    high = jnp.where(core == 0, other, own)
    total[...] = high[GRADS - 1]
    direct[...] = jnp.zeros_like(direct)
    for v in range(HELD * HALF):
        u, step = divmod(v, HALF)
        block = (9 * group + 4 * xl + u) // 16
        col = lax.rem(block + step, BLOCKS)
        direct[col, 8 * u : 8 * u + 8, :] = low[GRADS + v] if v < 13 else high[GRADS + v - 13]
    pad = jnp.zeros((128 - 8 * HELD, 128), F32)
    for col in range(BLOCKS):
        flat[128 * col : 128 * col + 128, :] = jnp.concatenate([direct[col], pad], axis=0).T
    flat[DA : DA + 8, :] = jnp.zeros((8, 128), F32)
    send[:, :GRADS] = jnp.broadcast_to(own[None, :GRADS], (CHIPS, GRADS, 8, 128))
    for here in (0, 1):

        @pl.when(core == here)
        def _():
            for n in range(CHIPS):
                first = 36 * n + 18 * here
                send[n, GRADS:] = flat[first : first + 24, :].reshape(3, 8, 128)


def spread(place, done, twin):
    vmem = pl.BlockSpec(memory_space=pltpu.VMEM)
    return pl.pallas_call(
        spread_kernel,
        out_shape=(
            jax.ShapeDtypeStruct((CHIPS, 2 * GRADS, 8, 128), F32),
            jax.ShapeDtypeStruct((BLOCKS, 8 * HELD, 128), F32),
            jax.ShapeDtypeStruct((8, 128), F32),
        ),
        in_specs=[pl.BlockSpec(memory_space=pltpu.SMEM), vmem, vmem],
        scratch_shapes=[pltpu.VMEM((DA + 8, 128), F32)],
        name="spread",
    )(place, done, twin)


def rows_kernel(place_ref, got, direct, total_ref, out, turned):
    group, xl, core = place_ref[0], place_ref[1], place_ref[2]
    total = total_ref[0:1, 0:1]
    for n in range(CHIPS):
        first = 4 * (n % 2)
        turned[:, 36 * n : 36 * n + 36] = got[n, GRADS:].reshape(24, 128)[:, first : first + 36]
    start = 72 * group + 36 * xl + 18 * core
    block = (lax.broadcasted_iota(jnp.int32, (18, 128), 0) + start) // 128
    for here in range(4):

        @pl.when(2 * xl + core == here)
        def _():
            first = 4 * (here // 2) + 18 * (here % 2)
            for col in range(BLOCKS):
                step = col - block
                step = jnp.where(step < 0, step + BLOCKS, step)
                lanes = slice(128 * col, 128 * col + 128)
                value = jnp.where(step < HALF, direct[col, first : first + 18, :], turned[:18, lanes]) / total
                for i in range(18):
                    out[i, :, lanes] = value[i : i + 1, :]


def factor_rows(place, got, direct, total):
    vmem = pl.BlockSpec(memory_space=pltpu.VMEM)
    out = pl.pallas_call(
        rows_kernel,
        out_shape=jax.ShapeDtypeStruct((18, 1, DA), F32),
        in_specs=[pl.BlockSpec(memory_space=pltpu.SMEM)] + [vmem] * 3,
        scratch_shapes=[pltpu.VMEM((24, DA), F32)],
        cost_estimate=pl.CostEstimate(flops=10**6, bytes_accessed=2**20, transcendentals=0),
        name="factor_rows",
    )(place, got, direct, total)
    return out.reshape(1, 18, DA)


def precond_kernel(place_ref, got, other, total_ref, basis_a, basis_g, eig_a, eig_g, g_factor, precond):
    core = place_ref[2]
    total = total_ref[0:1, 0:1]
    shape = (16, 2, 2 * GRADS, 8, 128)
    both = (got[...].reshape(shape), other[...].reshape(shape))
    columns = []
    for col in range(WIDTH // 128):
        n, rest = divmod(col, 5)
        low, rest = (rest < 3), (rest if rest < 3 else rest - 3)
        tiles = jnp.where((core == 0) == low, both[0][:, n, rest], both[1][:, n, rest])
        columns.append(tiles.reshape(128, 128) / total)
    g_factor[0] = columns[-1]
    grad = jnp.concatenate([c.astype(BF16) for c in columns[:-1]], axis=1)
    left = lax.dot_general(basis_g[0], grad, (((0,), (0,)), ((), ())), preferred_element_type=F32).astype(BF16)
    rotated = jnp.dot(left, basis_a[0], preferred_element_type=F32)
    eig_rows = jnp.broadcast_to(eig_g[...], (DG, DG)).T[:, 0:1]
    scaled = (rotated / (eig_rows * eig_a[...] + 0.001)).astype(BF16)
    inner = jnp.dot(basis_g[0], scaled, preferred_element_type=F32).astype(BF16)
    precond[0] = lax.dot_general(inner, basis_a[0], (((1,), (1,)), ((), ())), preferred_element_type=F32)


def precondition(place, got, other, total, basis_a, basis_g, eig_a, eig_g):
    vmem = pl.BlockSpec(memory_space=pltpu.VMEM)
    return pl.pallas_call(
        precond_kernel,
        out_shape=(jax.ShapeDtypeStruct((1, DG, DG), F32), jax.ShapeDtypeStruct((1, DG, DA), F32)),
        in_specs=[pl.BlockSpec(memory_space=pltpu.SMEM)] + [vmem] * 7,
        compiler_params=pltpu.CompilerParams(vmem_limit_bytes=40 * 2**20),
        name="precondition",
    )(place, got, other, total, basis_a, basis_g, eig_a, eig_g)


def swap_cores(value):
    return lax.ppermute(value, "core", [(0, 1), (1, 0)])


def on_device(patches, out_grads, counts, basis_a, basis_g, eig_a, eig_g):
    xl, core = lax.axis_index("xl"), lax.axis_index("core")
    place = jnp.stack([lax.axis_index(("zl", "y", "xh")), xl, core])
    mine, theirs = gram(patches, out_grads, counts, place)
    met = lax.all_to_all(mine + swap_cores(theirs), CHIP_AXES, 0, 0, tiled=True)
    copies = jnp.broadcast_to(jnp.sum(met, axis=0)[None], (4, SLOTS, 8, 128))
    done = jnp.sum(lax.all_to_all(copies, "zh", 0, 0, tiled=True), axis=0)
    send, direct, total = spread(place, done, swap_cores(done))
    got = lax.all_to_all(send, CHIP_AXES, 0, 0, tiled=True)
    other = swap_cores(got)
    a_factor = factor_rows(place, got, direct, total)
    g_factor, precond = precondition(place, got, other, total, basis_a, basis_g, eig_a, eig_g)
    return a_factor, g_factor, precond


def solution(mesh):
    axes = ("zl", "y", "xh", "xl", "core", "zh")
    finer = Mesh(mesh.devices.reshape(2, 4, 2, 2, 2, 4), axes)
    placed = (P(None, axes, None), P(None, axes, None), P(axes), P(), P(), P(), P())
    return jax.shard_map(
        on_device,
        mesh=finer,
        in_specs=placed,
        out_specs=(P(None, axes[:-1], None), P(), P()),
        check_vma=False,
    )
```

```python
import functools

import jax
import jax.numpy as jnp
from jax import lax
from jax.experimental import pallas as pl
from jax.experimental.pallas import tpu as pltpu
from jax.sharding import Mesh, PartitionSpec as P

DA, DG, ROWS = 1152, 128, 2048
WIDTH = DA + DG
BLOCKS = DA // 128
HALF = BLOCKS // 2 + 1
CHIPS, SLOTS, GRADS = 32, 16, 3
HELD = 5
CHIP_AXES = ("zl", "y", "xh", "xl")
HBM = pltpu.MemorySpace.HBM
F32, BF16 = jnp.float32, jnp.bfloat16


def factor_places(row8, step):
    group, within = divmod(row8, 9)
    for xl in (0, 1):
        v = (within - 4 * xl) * HALF + step
        if 0 <= within - 4 * xl < HELD:
            yield (0, 2 * group + xl, GRADS + v) if v < 13 else (1, 2 * group + xl, GRADS + v - 13)


def grad_place(row8, col):
    chip, rest = divmod(row8 * 10 + col, 5)
    return (0, chip, rest) if rest < 3 else (1, chip, rest - 3)


def position():
    group = (lax.axis_index("zl") * 4 + lax.axis_index("y")) * 2 + lax.axis_index("xh")
    return group, lax.axis_index("xl"), lax.axis_index("core")


def products(half, z, zt, acc):
    depth = slice(half * ROWS // 2, (half + 1) * ROWS // 2)

    def put(place, tile):
        acc[place] = acc[place] + tile if half else tile

    for col0 in range(0, BLOCKS + 1, 2):
        wanted = sorted({(c - s) % BLOCKS for c in (col0, col0 + 1) if c < BLOCKS for s in range(HALF)}) + [BLOCKS]
        runs = []
        for i in wanted:
            if runs and runs[-1][-1] == i - 1:
                runs[-1].append(i)
            else:
                runs.append([i])
        for run in runs:
            w = jnp.dot(
                zt[128 * run[0] : 128 * run[-1] + 128, depth],
                z[depth, 128 * col0 : 128 * col0 + 256],
                preferred_element_type=F32,
            )
            for u in range(16 * len(run)):
                row8 = 16 * run[0] + u
                for v in (0, 1):
                    tile = w[8 * u : 8 * u + 8, 128 * v : 128 * v + 128]
                    if row8 >= DA // 8:
                        put(grad_place(row8 - DA // 8, col0 + v), tile)
                    elif col0 + v < BLOCKS and (col0 + v - row8 // 16) % BLOCKS < HALF:
                        for place in factor_places(row8, (col0 + v - row8 // 16) % BLOCKS):
                            put(place, tile)


def gram_kernel(parts, count_ref, x_hbm, y_hbm, mine, theirs, z, zt, acc, in_sem, out_sem):
    step = ROWS // parts
    copies = []
    for k in range(parts):
        rows = pl.ds(k * step, step)
        copies.append(
            (
                pltpu.make_async_copy(x_hbm.at[0, rows, :], z.at[rows, pl.ds(0, DA)], in_sem.at[k, 0]),
                pltpu.make_async_copy(y_hbm.at[0, rows, :], z.at[rows, pl.ds(DA, DG)], in_sem.at[k, 1]),
            )
        )
        for copy in copies[k]:
            copy.start()
    count, core = count_ref[0], lax.axis_index("core")
    acc[1, :, SLOTS - 1, :, :] = jnp.zeros((CHIPS, 8, 128), F32)
    acc[1, :, GRADS - 1, :, :] = jnp.full((CHIPS, 8, 128), count.astype(F32))
    for half in (0, 1):
        for k in range(half * parts // 2, (half + 1) * parts // 2):
            for copy in copies[k]:
                copy.wait()
            here = slice(k * step, (k + 1) * step)
            row = lax.broadcasted_iota(jnp.int32, (step, 1), 0) + k * step
            zt[:, here] = jnp.where(row < count, z[here, :], jnp.zeros((), BF16)).T
        products(half, z, zt, acc)
    first = pltpu.make_async_copy(acc.at[1 - core], theirs, out_sem.at[0])
    second = pltpu.make_async_copy(acc.at[core], mine, out_sem.at[1])
    first.start()
    second.start()
    first.wait()
    second.wait()


def gram(patches, out_grads, counts):
    parts = 4
    half = jax.ShapeDtypeStruct((CHIPS, SLOTS, 8, 128), F32)
    return pl.pallas_call(
        functools.partial(gram_kernel, parts),
        out_shape=(half, half),
        in_specs=[pl.BlockSpec(memory_space=pltpu.SMEM)] + [pl.BlockSpec(memory_space=HBM)] * 2,
        out_specs=(pl.BlockSpec(memory_space=HBM),) * 2,
        scratch_shapes=[
            pltpu.VMEM((ROWS, WIDTH), BF16),
            pltpu.VMEM((WIDTH, ROWS), BF16),
            pltpu.VMEM((2, CHIPS, SLOTS, 8, 128), F32),
            pltpu.SemaphoreType.DMA((parts, 2)),
            pltpu.SemaphoreType.DMA((2,)),
        ],
        compiler_params=pltpu.CompilerParams(vmem_limit_bytes=48 * 2**20),
        cost_estimate=pl.CostEstimate(flops=2 * ROWS * WIDTH * WIDTH, bytes_accessed=10 * 2**20, transcendentals=0),
        name="gram",
    )(counts, patches, out_grads)


def spread_kernel(done, twin, send, direct, total, flat):
    group, xl, core = position()
    own, other = done[...], twin[...]
    low = jnp.where(core == 0, own, other)
    high = jnp.where(core == 0, other, own)
    total[...] = high[GRADS - 1]
    direct[...] = jnp.zeros_like(direct)
    for v in range(HELD * HALF):
        u, step = divmod(v, HALF)
        block = (9 * group + 4 * xl + u) // 16
        col = lax.rem(block + step, BLOCKS)
        direct[col, 8 * u : 8 * u + 8, :] = low[GRADS + v] if v < 13 else high[GRADS + v - 13]
    pad = jnp.zeros((128 - 8 * HELD, 128), F32)
    for col in range(BLOCKS):
        flat[0, 128 * col : 128 * col + 128, :] = jnp.concatenate([direct[col], pad], axis=0).T
    flat[0, DA : DA + 8, :] = jnp.zeros((8, 128), F32)
    for third in (1, 2):
        flat[third] = pltpu.roll(flat[0], 8 * HELD * third, 1)
    send[:, :GRADS] = jnp.broadcast_to(own[None, :GRADS], (CHIPS, GRADS, 8, 128))
    for here in (0, 1):

        @pl.when(core == here)
        def _():
            for n in range(CHIPS):
                first = 36 * n + 18 * here
                thirds = [flat[t, first + 6 * t : first + 6 * t + 8, :] for t in range(3)]
                send[n, GRADS] = thirds[0] + thirds[1] + thirds[2]


def spread(done, twin):
    vmem = pl.BlockSpec(memory_space=pltpu.VMEM)
    return pl.pallas_call(
        spread_kernel,
        out_shape=(
            jax.ShapeDtypeStruct((CHIPS, GRADS + 1, 8, 128), F32),
            jax.ShapeDtypeStruct((BLOCKS, 8 * HELD, 128), F32),
            jax.ShapeDtypeStruct((8, 128), F32),
        ),
        in_specs=[vmem, vmem],
        out_specs=(vmem,) * 3,
        scratch_shapes=[pltpu.VMEM((3, DA + 8, 128), F32)],
        compiler_params=pltpu.CompilerParams(vmem_limit_bytes=16 * 2**20),
        name="spread",
    )(done, twin)


def rows_kernel(got, direct, total_ref, out, turned):
    group, xl, core = position()
    total = total_ref[0:1, 0:1]
    for n in range(CHIPS):
        for third in range(3):
            first = 8 * HELD * third + 4 * (n % 2)
            turned[6 * third : 6 * third + 6, 36 * n : 36 * n + 36] = got[n, GRADS, 0:6, first : first + 36]
    start = 72 * group + 36 * xl + 18 * core
    block = (lax.broadcasted_iota(jnp.int32, (18, 128), 0) + start) // 128
    for here in range(4):

        @pl.when(2 * xl + core == here)
        def _():
            first = 4 * (here // 2) + 18 * (here % 2)
            for col in range(BLOCKS):
                step = col - block
                step = jnp.where(step < 0, step + BLOCKS, step)
                lanes = slice(128 * col, 128 * col + 128)
                value = jnp.where(step < HALF, direct[col, first : first + 18, :], turned[:18, lanes]) / total
                for i in range(18):
                    out[i, :, lanes] = value[i : i + 1, :]


def factor_rows(got, direct, total):
    vmem = pl.BlockSpec(memory_space=pltpu.VMEM)
    out = pl.pallas_call(
        rows_kernel,
        out_shape=jax.ShapeDtypeStruct((18, 1, DA), F32),
        in_specs=[vmem] * 3,
        scratch_shapes=[pltpu.VMEM((24, DA), F32)],
        compiler_params=pltpu.CompilerParams(vmem_limit_bytes=16 * 2**20),
        cost_estimate=pl.CostEstimate(flops=10**6, bytes_accessed=2**20, transcendentals=0),
        name="factor_rows",
    )(got, direct, total)
    return out.reshape(1, 18, DA)


def precond_kernel(got, other, total_ref, basis_a, basis_g, eig_a, eig_g, g_factor, precond):
    core = lax.axis_index("core")
    total = total_ref[0:1, 0:1]
    shape = (16, 2, GRADS + 1, 8, 128)
    both = (got[...].reshape(shape), other[...].reshape(shape))
    columns = []
    for col in range(WIDTH // 128):
        n, rest = divmod(col, 5)
        low, rest = (rest < 3), (rest if rest < 3 else rest - 3)
        tiles = jnp.where((core == 0) == low, both[0][:, n, rest], both[1][:, n, rest])
        columns.append(tiles.reshape(128, 128) / total)
    g_factor[0] = columns[-1]
    grad = jnp.concatenate([c.astype(BF16) for c in columns[:-1]], axis=1)
    left = lax.dot_general(basis_g[0], grad, (((0,), (0,)), ((), ())), preferred_element_type=F32).astype(BF16)
    rotated = jnp.dot(left, basis_a[0], preferred_element_type=F32)
    eig_rows = jnp.broadcast_to(eig_g[...], (DG, DG)).T[:, 0:1]
    scaled = (rotated / (eig_rows * eig_a[...] + 0.001)).astype(BF16)
    inner = jnp.dot(basis_g[0], scaled, preferred_element_type=F32).astype(BF16)
    precond[0] = lax.dot_general(inner, basis_a[0], (((1,), (1,)), ((), ())), preferred_element_type=F32)


def precondition(got, other, total, basis_a, basis_g, eig_a, eig_g):
    vmem = pl.BlockSpec(memory_space=pltpu.VMEM)
    return pl.pallas_call(
        precond_kernel,
        out_shape=(jax.ShapeDtypeStruct((1, DG, DG), F32), jax.ShapeDtypeStruct((1, DG, DA), F32)),
        in_specs=[vmem] * 7,
        compiler_params=pltpu.CompilerParams(vmem_limit_bytes=40 * 2**20),
        name="precondition",
    )(got, other, total, basis_a, basis_g, eig_a, eig_g)


def swap_cores(value):
    return lax.ppermute(value, "core", [(0, 1), (1, 0)])


def group_sum(value):
    first, second, third = (lax.ppermute(value, "zh", [(i, i ^ k) for i in range(4)]) for k in (1, 2, 3))
    return (value + first) + (second + third)


def on_device(patches, out_grads, counts, basis_a, basis_g, eig_a, eig_g):
    mine, theirs = gram(patches, out_grads, counts)
    met = lax.all_to_all(mine + swap_cores(theirs), CHIP_AXES, 0, 0, tiled=True)
    done = group_sum(jnp.sum(met, axis=0))
    send, direct, total = spread(done, swap_cores(done))
    got = lax.all_to_all(send, CHIP_AXES, 0, 0, tiled=True)
    other = swap_cores(got)
    a_factor = factor_rows(got, direct, total)
    g_factor, precond = precondition(got, other, total, basis_a, basis_g, eig_a, eig_g)
    return a_factor, g_factor, precond


def solution(mesh):
    axes = ("zl", "y", "xh", "xl", "core", "zh")
    finer = Mesh(mesh.devices.reshape(2, 4, 2, 2, 2, 4), axes)
    placed = (P(None, axes, None), P(None, axes, None), P(axes), P(), P(), P(), P())
    return jax.shard_map(
        on_device,
        mesh=finer,
        in_specs=placed,
        out_specs=(P(None, axes[:-1], None), P(), P()),
        check_vma=False,
    )
```

```python
import functools

import jax
import jax.numpy as jnp
from jax import lax
from jax.experimental import pallas as pl
from jax.experimental.pallas import tpu as pltpu
from jax.sharding import Mesh, PartitionSpec as P

DA, DG, ROWS = 1152, 128, 2048
WIDTH = DA + DG
BLOCKS = DA // 128
HALF = BLOCKS // 2 + 1
CHIPS, SLOTS, GRADS = 32, 16, 3
HELD = 5
CHIP_AXES = ("zl", "y", "x")
HBM = pltpu.MemorySpace.HBM
F32, BF16 = jnp.float32, jnp.bfloat16


def factor_places(row8, step):
    group, within = divmod(row8, 9)
    for xl in (0, 1):
        v = (within - 4 * xl) * HALF + step
        if 0 <= within - 4 * xl < HELD:
            yield (0, 2 * group + xl, GRADS + v) if v < 13 else (1, 2 * group + xl, GRADS + v - 13)


def grad_place(row8, col):
    chip, rest = divmod(row8 * 10 + col, 5)
    return (0, chip, rest) if rest < 3 else (1, chip, rest - 3)


def position():
    x = lax.axis_index("x")
    group = (lax.axis_index("zl") * 4 + lax.axis_index("y")) * 2 + lax.div(x, 2)
    return group, lax.rem(x, 2), lax.axis_index("core")


def chunked(core, chip, slot):
    zl, y, x = chip // 16, chip // 4 % 4, chip % 4
    half, slot = divmod(slot, SLOTS // 2)
    return (core, half) + ((y, x) if half else (x, y)) + (zl, slot)


def products(half, z, zt, acc):
    depth = slice(half * ROWS // 2, (half + 1) * ROWS // 2)

    def put(place, tile):
        place = chunked(*place)
        acc[place] = acc[place] + tile if half else tile

    for col0 in range(0, BLOCKS + 1, 2):
        wanted = sorted({(c - s) % BLOCKS for c in (col0, col0 + 1) if c < BLOCKS for s in range(HALF)}) + [BLOCKS]
        runs = []
        for i in wanted:
            if runs and runs[-1][-1] == i - 1:
                runs[-1].append(i)
            else:
                runs.append([i])
        for run in runs:
            w = jnp.dot(
                zt[128 * run[0] : 128 * run[-1] + 128, depth],
                z[depth, 128 * col0 : 128 * col0 + 256],
                preferred_element_type=F32,
            )
            for u in range(16 * len(run)):
                row8 = 16 * run[0] + u
                for v in (0, 1):
                    tile = w[8 * u : 8 * u + 8, 128 * v : 128 * v + 128]
                    if row8 >= DA // 8:
                        put(grad_place(row8 - DA // 8, col0 + v), tile)
                    elif col0 + v < BLOCKS and (col0 + v - row8 // 16) % BLOCKS < HALF:
                        for place in factor_places(row8, (col0 + v - row8 // 16) % BLOCKS):
                            put(place, tile)


def gram_kernel(parts, count_ref, x_hbm, y_hbm, mine0, mine1, theirs0, theirs1, z, zt, acc, in_sem, out_sem):
    step = ROWS // parts
    copies = []
    for k in range(parts):
        rows = pl.ds(k * step, step)
        copies.append(
            (
                pltpu.make_async_copy(x_hbm.at[0, rows, :], z.at[rows, pl.ds(0, DA)], in_sem.at[k, 0]),
                pltpu.make_async_copy(y_hbm.at[0, rows, :], z.at[rows, pl.ds(DA, DG)], in_sem.at[k, 1]),
            )
        )
        for copy in copies[k]:
            copy.start()
    count, core = count_ref[0], lax.axis_index("core")
    acc[1, 1, :, :, :, SLOTS // 2 - 1] = jnp.zeros((4, 4, 2, 8, 128), F32)
    acc[1, 0, :, :, :, GRADS - 1] = jnp.full((4, 4, 2, 8, 128), count.astype(F32))
    for half in (0, 1):
        for k in range(half * parts // 2, (half + 1) * parts // 2):
            for copy in copies[k]:
                copy.wait()
            here = slice(k * step, (k + 1) * step)
            row = lax.broadcasted_iota(jnp.int32, (step, 1), 0) + k * step
            zt[:, here] = jnp.where(row < count, z[here, :], jnp.zeros((), BF16)).T
        products(half, z, zt, acc)
    here = (lax.axis_index("x"), lax.axis_index("y"))
    waits = []
    for i, (which, half, out) in enumerate(((1 - core, 0, theirs0), (1 - core, 1, theirs1), (core, 0, mine0), (core, 1, mine1))):
        for a in range(4):
            for b in range(4):
                source = acc.at[which, half, here[half] ^ a, here[1 - half] ^ b]
                pltpu.make_async_copy(source, out.at[a, b], out_sem.at[i]).start()
        waits.append(pltpu.make_async_copy(acc.at[which, half], out, out_sem.at[i]))
    for wait in waits:
        wait.wait()


def gram(patches, out_grads, counts):
    parts = 4
    half = jax.ShapeDtypeStruct((4, 4, 2, SLOTS // 2, 8, 128), F32)
    return pl.pallas_call(
        functools.partial(gram_kernel, parts),
        out_shape=(half,) * 4,
        in_specs=[pl.BlockSpec(memory_space=pltpu.SMEM)] + [pl.BlockSpec(memory_space=HBM)] * 2,
        out_specs=(pl.BlockSpec(memory_space=HBM),) * 4,
        scratch_shapes=[
            pltpu.VMEM((ROWS, WIDTH), BF16),
            pltpu.VMEM((WIDTH, ROWS), BF16),
            pltpu.VMEM((2, 2, 4, 4, 2, SLOTS // 2, 8, 128), F32),
            pltpu.SemaphoreType.DMA((parts, 2)),
            pltpu.SemaphoreType.DMA((4,)),
        ],
        compiler_params=pltpu.CompilerParams(vmem_limit_bytes=48 * 2**20),
        cost_estimate=pl.CostEstimate(flops=2 * ROWS * WIDTH * WIDTH, bytes_accessed=10 * 2**20, transcendentals=0),
        name="gram",
    )(counts, patches, out_grads)


def spread_kernel(done, twin, send, direct, total, flat):
    group, xl, core = position()
    own, other = done[...], twin[...]
    low = jnp.where(core == 0, own, other)
    high = jnp.where(core == 0, other, own)
    total[...] = high[GRADS - 1]
    direct[...] = jnp.zeros_like(direct)
    for v in range(HELD * HALF):
        u, step = divmod(v, HALF)
        block = (9 * group + 4 * xl + u) // 16
        col = lax.rem(block + step, BLOCKS)
        direct[col, 8 * u : 8 * u + 8, :] = low[GRADS + v] if v < 13 else high[GRADS + v - 13]
    pad = jnp.zeros((128 - 8 * HELD, 128), F32)
    for col in range(BLOCKS):
        flat[0, 128 * col : 128 * col + 128, :] = jnp.concatenate([direct[col], pad], axis=0).T
    flat[0, DA : DA + 8, :] = jnp.zeros((8, 128), F32)
    for third in (1, 2):
        flat[third] = pltpu.roll(flat[0], 8 * HELD * third, 1)
    send[:, :GRADS] = jnp.broadcast_to(own[None, :GRADS], (CHIPS, GRADS, 8, 128))
    for here in (0, 1):

        @pl.when(core == here)
        def _():
            for n in range(CHIPS):
                first = 36 * n + 18 * here
                thirds = [flat[t, first + 6 * t : first + 6 * t + 8, :] for t in range(3)]
                send[n, GRADS] = thirds[0] + thirds[1] + thirds[2]


def spread(done, twin):
    vmem = pl.BlockSpec(memory_space=pltpu.VMEM)
    return pl.pallas_call(
        spread_kernel,
        out_shape=(
            jax.ShapeDtypeStruct((CHIPS, GRADS + 1, 8, 128), F32),
            jax.ShapeDtypeStruct((BLOCKS, 8 * HELD, 128), F32),
            jax.ShapeDtypeStruct((8, 128), F32),
        ),
        in_specs=[vmem, vmem],
        out_specs=(vmem,) * 3,
        scratch_shapes=[pltpu.VMEM((3, DA + 8, 128), F32)],
        compiler_params=pltpu.CompilerParams(vmem_limit_bytes=16 * 2**20),
        name="spread",
    )(done, twin)


def rows_kernel(got, direct, total_ref, out, turned):
    group, xl, core = position()
    total = total_ref[0:1, 0:1]
    for n in range(CHIPS):
        for third in range(3):
            first = 8 * HELD * third + 4 * (n % 2)
            turned[6 * third : 6 * third + 6, 36 * n : 36 * n + 36] = got[n, GRADS, 0:6, first : first + 36]
    start = 72 * group + 36 * xl + 18 * core
    block = (lax.broadcasted_iota(jnp.int32, (18, 128), 0) + start) // 128
    for here in range(4):

        @pl.when(2 * xl + core == here)
        def _():
            first = 4 * (here // 2) + 18 * (here % 2)
            for col in range(BLOCKS):
                step = col - block
                step = jnp.where(step < 0, step + BLOCKS, step)
                lanes = slice(128 * col, 128 * col + 128)
                value = jnp.where(step < HALF, direct[col, first : first + 18, :], turned[:18, lanes]) / total
                for i in range(18):
                    out[i, :, lanes] = value[i : i + 1, :]


def factor_rows(got, direct, total):
    vmem = pl.BlockSpec(memory_space=pltpu.VMEM)
    out = pl.pallas_call(
        rows_kernel,
        out_shape=jax.ShapeDtypeStruct((18, 1, DA), F32),
        in_specs=[vmem] * 3,
        scratch_shapes=[pltpu.VMEM((24, DA), F32)],
        compiler_params=pltpu.CompilerParams(vmem_limit_bytes=16 * 2**20),
        cost_estimate=pl.CostEstimate(flops=10**6, bytes_accessed=2**20, transcendentals=0),
        name="factor_rows",
    )(got, direct, total)
    return out.reshape(1, 18, DA)


def precond_kernel(got, other, total_ref, basis_a, basis_g, eig_a, eig_g, g_factor, precond):
    core = lax.axis_index("core")
    total = total_ref[0:1, 0:1]
    shape = (16, 2, GRADS + 1, 8, 128)
    both = (got[...].reshape(shape), other[...].reshape(shape))
    columns = []
    for col in range(WIDTH // 128):
        n, rest = divmod(col, 5)
        low, rest = (rest < 3), (rest if rest < 3 else rest - 3)
        tiles = jnp.where((core == 0) == low, both[0][:, n, rest], both[1][:, n, rest])
        columns.append(tiles.reshape(128, 128) / total)
    g_factor[0] = columns[-1]
    grad = jnp.concatenate([c.astype(BF16) for c in columns[:-1]], axis=1)
    left = lax.dot_general(basis_g[0], grad, (((0,), (0,)), ((), ())), preferred_element_type=F32).astype(BF16)
    rotated = jnp.dot(left, basis_a[0], preferred_element_type=F32)
    eig_rows = jnp.broadcast_to(eig_g[...], (DG, DG)).T[:, 0:1]
    scaled = (rotated / (eig_rows * eig_a[...] + 0.001)).astype(BF16)
    inner = jnp.dot(basis_g[0], scaled, preferred_element_type=F32).astype(BF16)
    precond[0] = lax.dot_general(inner, basis_a[0], (((1,), (1,)), ((), ())), preferred_element_type=F32)


def precondition(got, other, total, basis_a, basis_g, eig_a, eig_g):
    vmem = pl.BlockSpec(memory_space=pltpu.VMEM)
    return pl.pallas_call(
        precond_kernel,
        out_shape=(jax.ShapeDtypeStruct((1, DG, DG), F32), jax.ShapeDtypeStruct((1, DG, DA), F32)),
        in_specs=[vmem] * 7,
        compiler_params=pltpu.CompilerParams(vmem_limit_bytes=40 * 2**20),
        name="precondition",
    )(got, other, total, basis_a, basis_g, eig_a, eig_g)


def swap_cores(value):
    return lax.ppermute(value, "core", [(0, 1), (1, 0)])


def meet(value, axis, distance):
    return lax.ppermute(value, axis, [(i, i ^ distance) for i in range(4)])


def sum_first(value, axis):
    first, second, third = (meet(value[k], axis, k) for k in (1, 2, 3))
    return (value[0] + first) + (second + third)


def sum_second(value, axis):
    got = meet(value[1:3], axis, 1)
    return (value[0] + got[0]) + meet(value[3] + got[1], axis, 3)


def group_sum(value):
    first, second, third = (meet(value, "zh", k) for k in (1, 2, 3))
    return (value + first) + (second + third)


def on_device(patches, out_grads, counts, basis_a, basis_g, eig_a, eig_g):
    mine0, mine1, theirs0, theirs1 = gram(patches, out_grads, counts)
    other0, other1 = swap_cores(theirs0), swap_cores(theirs1)
    half0, half1 = sum_first(mine0 + other0, "x"), sum_first(mine1 + other1, "y")
    half0, half1 = sum_second(half0, "y"), sum_second(half1, "x")
    both = jnp.concatenate([half0, half1], axis=1)
    low = lax.axis_index("zl") == 0
    away = lax.ppermute(jnp.where(low, both[1], both[0]), "zl", [(0, 1), (1, 0)])
    done = group_sum(jnp.where(low, both[0], both[1]) + away)
    send, direct, total = spread(done, swap_cores(done))
    got = lax.all_to_all(send, CHIP_AXES, 0, 0, tiled=True)
    other = swap_cores(got)
    a_factor = factor_rows(got, direct, total)
    g_factor, precond = precondition(got, other, total, basis_a, basis_g, eig_a, eig_g)
    return a_factor, g_factor, precond


def solution(mesh):
    axes = ("zl", "y", "x", "core", "zh")
    finer = Mesh(mesh.devices.reshape(2, 4, 4, 2, 4), axes)
    placed = (P(None, axes, None), P(None, axes, None), P(axes), P(), P(), P(), P())
    return jax.shard_map(
        on_device,
        mesh=finer,
        in_specs=placed,
        out_specs=(P(None, axes[:-1], None), P(), P()),
        check_vma=False,
    )
```

```python
import functools

import jax
import jax.numpy as jnp
from jax import lax
from jax.experimental import pallas as pl
from jax.experimental.pallas import tpu as pltpu
from jax.sharding import Mesh, PartitionSpec as P

DA, DG, ROWS = 1152, 128, 2048
WIDTH = DA + DG
BLOCKS = DA // 128
HALF = BLOCKS // 2 + 1
CHIPS, SLOTS, GRADS = 32, 14, 3
LOW = SLOTS - GRADS
CHIP_AXES = ("zl", "y", "xh", "xl")
HBM = pltpu.MemorySpace.HBM
F32, BF16 = jnp.float32, jnp.bfloat16


def factor_slot(v):
    return (0, GRADS + v) if v < LOW else (1, GRADS - 1 + v - LOW)


def factor_places(row8, step):
    group, within = divmod(row8, 9)
    if within == 4:
        core, slot = factor_slot(4 * HALF + step // 2)
        to = slice(4 * (step % 2), 4 * (step % 2) + 4)
        for xl in (0, 1):
            yield (core, 2 * group + xl, slot, to), slice(4 * xl, 4 * xl + 4)
    else:
        xl = within // 5
        core, slot = factor_slot((within - 5 * xl) * HALF + step)
        yield (core, 2 * group + xl, slot, slice(0, 8)), slice(0, 8)


def grad_place(row8, col):
    chip, rest = divmod(row8 * 10 + col, 5)
    return (0, chip, rest, slice(0, 8)) if rest < 3 else (1, chip, rest - 3, slice(0, 8))


def position():
    group = (lax.axis_index("zl") * 4 + lax.axis_index("y")) * 2 + lax.axis_index("xh")
    return group, lax.axis_index("xl"), lax.axis_index("core")


def products(half, z, zt, acc):
    depth = slice(half * ROWS // 2, (half + 1) * ROWS // 2)

    def put(place, tile):
        acc[place] = acc[place] + tile if half else tile

    for col0 in range(0, BLOCKS + 1, 2):
        wanted = sorted({(c - s) % BLOCKS for c in (col0, col0 + 1) if c < BLOCKS for s in range(HALF)}) + [BLOCKS]
        runs = []
        for i in wanted:
            if runs and runs[-1][-1] == i - 1:
                runs[-1].append(i)
            else:
                runs.append([i])
        for run in runs:
            w = jnp.dot(
                zt[128 * run[0] : 128 * run[-1] + 128, depth],
                z[depth, 128 * col0 : 128 * col0 + 256],
                preferred_element_type=F32,
            )
            for u in range(16 * len(run)):
                row8 = 16 * run[0] + u
                for v in (0, 1):
                    tile = w[8 * u : 8 * u + 8, 128 * v : 128 * v + 128]
                    if row8 >= DA // 8:
                        put(grad_place(row8 - DA // 8, col0 + v), tile)
                    elif col0 + v < BLOCKS and (col0 + v - row8 // 16) % BLOCKS < HALF:
                        for place, rows in factor_places(row8, (col0 + v - row8 // 16) % BLOCKS):
                            put(place, tile[rows])


def gram_kernel(parts, count_ref, x_hbm, y_hbm, mine, theirs, z, zt, acc, in_sem, out_sem):
    step = ROWS // parts
    copies = []
    for k in range(parts):
        rows = pl.ds(k * step, step)
        copies.append(
            (
                pltpu.make_async_copy(x_hbm.at[0, rows, :], z.at[rows, pl.ds(0, DA)], in_sem.at[k, 0]),
                pltpu.make_async_copy(y_hbm.at[0, rows, :], z.at[rows, pl.ds(DA, DG)], in_sem.at[k, 1]),
            )
        )
        for copy in copies[k]:
            copy.start()
    count, core = count_ref[0], lax.axis_index("core")
    acc[1, :, SLOTS - 1, 4:8, :] = jnp.full((CHIPS, 4, 128), count.astype(F32))
    for half in (0, 1):
        for k in range(half * parts // 2, (half + 1) * parts // 2):
            for copy in copies[k]:
                copy.wait()
            here = slice(k * step, (k + 1) * step)
            row = lax.broadcasted_iota(jnp.int32, (step, 1), 0) + k * step
            zt[:, here] = jnp.where(row < count, z[here, :], jnp.zeros((), BF16)).T
        products(half, z, zt, acc)
    first = pltpu.make_async_copy(acc.at[1 - core], theirs, out_sem.at[0])
    second = pltpu.make_async_copy(acc.at[core], mine, out_sem.at[1])
    first.start()
    second.start()
    first.wait()
    second.wait()


def gram(patches, out_grads, counts):
    parts = 4
    half = jax.ShapeDtypeStruct((CHIPS, SLOTS, 8, 128), F32)
    return pl.pallas_call(
        functools.partial(gram_kernel, parts),
        out_shape=(half, half),
        in_specs=[pl.BlockSpec(memory_space=pltpu.SMEM)] + [pl.BlockSpec(memory_space=HBM)] * 2,
        out_specs=(pl.BlockSpec(memory_space=HBM),) * 2,
        scratch_shapes=[
            pltpu.VMEM((ROWS, WIDTH), BF16),
            pltpu.VMEM((WIDTH, ROWS), BF16),
            pltpu.VMEM((2, CHIPS, SLOTS, 8, 128), F32),
            pltpu.SemaphoreType.DMA((parts, 2)),
            pltpu.SemaphoreType.DMA((2,)),
        ],
        compiler_params=pltpu.CompilerParams(vmem_limit_bytes=48 * 2**20),
        cost_estimate=pl.CostEstimate(flops=2 * ROWS * WIDTH * WIDTH, bytes_accessed=10 * 2**20, transcendentals=0),
        name="gram",
    )(counts, patches, out_grads)


def collect_kernel(met, out):
    total = met[0]
    for n in range(1, CHIPS):
        total = total + met[n]
    out[...] = total


def collect(met):
    return pl.pallas_call(
        collect_kernel,
        out_shape=jax.ShapeDtypeStruct((SLOTS, 8, 128), F32),
        compiler_params=pltpu.CompilerParams(vmem_limit_bytes=16 * 2**20),
        name="collect",
    )(met)


def spread_kernel(done, twin, send, direct, total, flat):
    group, xl, core = position()
    own, other = done[...], twin[...]
    low = jnp.where(core == 0, own, other)
    high = jnp.where(core == 0, other, own)
    total[...] = jnp.broadcast_to(high[SLOTS - 1, 4:5], (8, 128))
    direct[...] = jnp.zeros_like(direct)
    shared = (9 * group + 4) // 16
    for v in range(4 * HALF + HALF // 2 + 1):
        here, slot = factor_slot(v)
        tile = high[slot] if here else low[slot]
        u, step = divmod(v, HALF)
        if u < 4:
            col = lax.rem((9 * group + 5 * xl + u) // 16 + step, BLOCKS)
            direct[col, 8 * u : 8 * u + 8, :] = tile
        else:
            direct[lax.rem(shared + 2 * step, BLOCKS), 32:36, :] = tile[0:4]
            if 2 * step + 1 < HALF:
                direct[lax.rem(shared + 2 * step + 1, BLOCKS), 32:36, :] = tile[4:8]
    pad = jnp.zeros((128 - 40, 128), F32)
    for col in range(BLOCKS):
        flat[0, 128 * col : 128 * col + 128, :] = jnp.concatenate([direct[col], pad], axis=0).T
    flat[0, DA : DA + 8, :] = jnp.zeros((8, 128), F32)
    for third in (1, 2):
        flat[third] = pltpu.roll(flat[0], 40 * third, 1)
    send[:, :GRADS] = jnp.broadcast_to(own[None, :GRADS], (CHIPS, GRADS, 8, 128))
    for here in (0, 1):

        @pl.when(core == here)
        def _():
            for n in range(CHIPS):
                first = 36 * n + 18 * here
                thirds = [flat[t, first + 6 * t : first + 6 * t + 8, :] for t in range(3)]
                send[n, GRADS] = thirds[0] + thirds[1] + thirds[2]


def spread(done, twin):
    vmem = pl.BlockSpec(memory_space=pltpu.VMEM)
    return pl.pallas_call(
        spread_kernel,
        out_shape=(
            jax.ShapeDtypeStruct((CHIPS, GRADS + 1, 8, 128), F32),
            jax.ShapeDtypeStruct((BLOCKS, 40, 128), F32),
            jax.ShapeDtypeStruct((8, 128), F32),
        ),
        in_specs=[vmem, vmem],
        out_specs=(vmem,) * 3,
        scratch_shapes=[pltpu.VMEM((3, DA + 8, 128), F32)],
        compiler_params=pltpu.CompilerParams(vmem_limit_bytes=16 * 2**20),
        name="spread",
    )(done, twin)


def rows_kernel(got, direct, total_ref, out, turned):
    group, xl, core = position()
    total = total_ref[0:1, 0:1]
    for n in range(CHIPS):
        for third in range(3):
            rows = slice(6 * third, 6 * third + 6)
            for to, first, size in ((4, 0, 32), (0, 32, 4)) if n % 2 else ((0, 0, 36),):
                first = first + 40 * third
                turned[rows, 36 * n + to : 36 * n + to + size] = got[n, GRADS, 0:6, first : first + size]
    start = 72 * group + 36 * xl + 18 * core
    block = (lax.broadcasted_iota(jnp.int32, (18, 128), 0) + start) // 128
    for here in range(4):

        @pl.when(2 * xl + core == here)
        def _():
            first = (0, 18, 0, 14)[here]
            for col in range(BLOCKS):
                step = col - block
                step = jnp.where(step < 0, step + BLOCKS, step)
                lanes = slice(128 * col, 128 * col + 128)
                if here == 2:
                    straight = jnp.concatenate([direct[col, 32:36, :], direct[col, 0:14, :]], axis=0)
                else:
                    straight = direct[col, first : first + 18, :]
                value = jnp.where(step < HALF, straight, turned[:18, lanes]) / total
                for i in range(18):
                    out[i, :, lanes] = value[i : i + 1, :]


def factor_rows(got, direct, total):
    vmem = pl.BlockSpec(memory_space=pltpu.VMEM)
    out = pl.pallas_call(
        rows_kernel,
        out_shape=jax.ShapeDtypeStruct((18, 1, DA), F32),
        in_specs=[vmem] * 3,
        scratch_shapes=[pltpu.VMEM((24, DA), F32)],
        compiler_params=pltpu.CompilerParams(vmem_limit_bytes=16 * 2**20),
        cost_estimate=pl.CostEstimate(flops=10**6, bytes_accessed=2**20, transcendentals=0),
        name="factor_rows",
    )(got, direct, total)
    return out.reshape(1, 18, DA)


def precond_kernel(got, other, total_ref, basis_a, basis_g, eig_a, eig_g, g_factor, precond):
    core = lax.axis_index("core")
    total = total_ref[0:1, 0:1]
    shape = (16, 2, GRADS + 1, 8, 128)
    both = (got[...].reshape(shape), other[...].reshape(shape))
    columns = []
    for col in range(WIDTH // 128):
        n, rest = divmod(col, 5)
        low, rest = (rest < 3), (rest if rest < 3 else rest - 3)
        tiles = jnp.where((core == 0) == low, both[0][:, n, rest], both[1][:, n, rest])
        columns.append(tiles.reshape(128, 128) / total)
    g_factor[0] = columns[-1]
    grad = jnp.concatenate([c.astype(BF16) for c in columns[:-1]], axis=1)
    left = lax.dot_general(basis_g[0], grad, (((0,), (0,)), ((), ())), preferred_element_type=F32).astype(BF16)
    rotated = jnp.dot(left, basis_a[0], preferred_element_type=F32)
    eig_rows = jnp.broadcast_to(eig_g[...], (DG, DG)).T[:, 0:1]
    scaled = (rotated / (eig_rows * eig_a[...] + 0.001)).astype(BF16)
    inner = jnp.dot(basis_g[0], scaled, preferred_element_type=F32).astype(BF16)
    precond[0] = lax.dot_general(inner, basis_a[0], (((1,), (1,)), ((), ())), preferred_element_type=F32)


def precondition(got, other, total, basis_a, basis_g, eig_a, eig_g):
    vmem = pl.BlockSpec(memory_space=pltpu.VMEM)
    return pl.pallas_call(
        precond_kernel,
        out_shape=(jax.ShapeDtypeStruct((1, DG, DG), F32), jax.ShapeDtypeStruct((1, DG, DA), F32)),
        in_specs=[vmem] * 7,
        compiler_params=pltpu.CompilerParams(vmem_limit_bytes=16 * 2**20),
        name="precondition",
    )(got, other, total, basis_a, basis_g, eig_a, eig_g)


def swap_cores(value):
    return lax.ppermute(value, "core", [(0, 1), (1, 0)])


def group_sum(value):
    first, second, third = (lax.ppermute(value, "zh", [(i, i ^ k) for i in range(4)]) for k in (1, 2, 3))
    return (value + first) + (second + third)


def on_device(patches, out_grads, counts, basis_a, basis_g, eig_a, eig_g):
    mine, theirs = gram(patches, out_grads, counts)
    met = lax.all_to_all(mine + swap_cores(theirs), CHIP_AXES, 0, 0, tiled=True)
    done = group_sum(collect(met))
    send, direct, total = spread(done, swap_cores(done))
    got = lax.all_to_all(send, CHIP_AXES, 0, 0, tiled=True)
    other = swap_cores(got)
    a_factor = factor_rows(got, direct, total)
    g_factor, precond = precondition(got, other, total, basis_a, basis_g, eig_a, eig_g)
    return a_factor, g_factor, precond


def solution(mesh):
    axes = ("zl", "y", "xh", "xl", "core", "zh")
    finer = Mesh(mesh.devices.reshape(2, 4, 2, 2, 2, 4), axes)
    placed = (P(None, axes, None), P(None, axes, None), P(axes), P(), P(), P(), P())
    return jax.shard_map(
        on_device,
        mesh=finer,
        in_specs=placed,
        out_specs=(P(None, axes[:-1], None), P(), P()),
        check_vma=False,
    )
```

```python
import functools

import jax
import jax.numpy as jnp
from jax import lax
from jax.experimental import pallas as pl
from jax.experimental.pallas import tpu as pltpu
from jax.sharding import Mesh, PartitionSpec as P

DA, DG, ROWS = 1152, 128, 2048
WIDTH = DA + DG
BLOCKS = DA // 128
HALF = BLOCKS // 2 + 1
CHIPS, SLOTS, GRADS = 32, 14, 3
LOW = SLOTS - GRADS
CHIP_AXES = ("zl", "y", "xh", "xl")
HBM = pltpu.MemorySpace.HBM
F32, BF16 = jnp.float32, jnp.bfloat16


def factor_slot(v):
    return (0, GRADS + v) if v < LOW else (1, GRADS - 1 + v - LOW)


def factor_places(row8, step):
    group, within = divmod(row8, 9)
    if within == 4:
        core, slot = factor_slot(4 * HALF + step // 2)
        to = slice(4 * (step % 2), 4 * (step % 2) + 4)
        for xl in (0, 1):
            yield (core, 2 * group + xl, slot, to), slice(4 * xl, 4 * xl + 4)
    else:
        xl = within // 5
        core, slot = factor_slot((within - 5 * xl) * HALF + step)
        yield (core, 2 * group + xl, slot, slice(0, 8)), slice(0, 8)


def grad_place(row8, col):
    chip, rest = divmod(row8 * 10 + col, 5)
    return (0, chip, rest, slice(0, 8)) if rest < 3 else (1, chip, rest - 3, slice(0, 8))


def position():
    group = (lax.axis_index("zl") * 4 + lax.axis_index("y")) * 2 + lax.axis_index("xh")
    return group, lax.axis_index("xl"), lax.axis_index("core")


def products(half, z, zt, acc):
    depth = slice(half * ROWS // 2, (half + 1) * ROWS // 2)

    def put(place, tile):
        acc[place] = acc[place] + tile if half else tile

    for col0 in range(0, BLOCKS + 1, 2):
        wanted = sorted({(c - s) % BLOCKS for c in (col0, col0 + 1) if c < BLOCKS for s in range(HALF)}) + [BLOCKS]
        runs = []
        for i in wanted:
            if runs and runs[-1][-1] == i - 1:
                runs[-1].append(i)
            else:
                runs.append([i])
        for run in runs:
            w = jnp.dot(
                zt[128 * run[0] : 128 * run[-1] + 128, depth],
                z[depth, 128 * col0 : 128 * col0 + 256],
                preferred_element_type=F32,
            )
            for u in range(16 * len(run)):
                row8 = 16 * run[0] + u
                for v in (0, 1):
                    tile = w[8 * u : 8 * u + 8, 128 * v : 128 * v + 128]
                    if row8 >= DA // 8:
                        put(grad_place(row8 - DA // 8, col0 + v), tile)
                    elif col0 + v < BLOCKS and (col0 + v - row8 // 16) % BLOCKS < HALF:
                        for place, rows in factor_places(row8, (col0 + v - row8 // 16) % BLOCKS):
                            put(place, tile[rows])


def gram_kernel(parts, count_ref, x_hbm, y_hbm, mine, theirs, z, zt, acc, in_sem, out_sem):
    step = ROWS // parts
    copies = []
    for k in range(parts):
        rows = pl.ds(k * step, step)
        copies.append(
            (
                pltpu.make_async_copy(x_hbm.at[0, rows, :], z.at[rows, pl.ds(0, DA)], in_sem.at[k, 0]),
                pltpu.make_async_copy(y_hbm.at[0, rows, :], z.at[rows, pl.ds(DA, DG)], in_sem.at[k, 1]),
            )
        )
        for copy in copies[k]:
            copy.start()
    count, core = count_ref[0], lax.axis_index("core")
    acc[1, :, SLOTS - 1, 4:8, :] = jnp.full((CHIPS, 4, 128), count.astype(F32))
    for half in (0, 1):
        for k in range(half * parts // 2, (half + 1) * parts // 2):
            for copy in copies[k]:
                copy.wait()
            here = slice(k * step, (k + 1) * step)
            row = lax.broadcasted_iota(jnp.int32, (step, 1), 0) + k * step
            zt[:, here] = jnp.where(row < count, z[here, :], jnp.zeros((), BF16)).T
        products(half, z, zt, acc)
    first = pltpu.make_async_copy(acc.at[1 - core], theirs, out_sem.at[0])
    second = pltpu.make_async_copy(acc.at[core], mine, out_sem.at[1])
    first.start()
    second.start()
    first.wait()
    second.wait()


def gram(patches, out_grads, counts):
    parts = 2
    half = jax.ShapeDtypeStruct((CHIPS, SLOTS, 8, 128), F32)
    return pl.pallas_call(
        functools.partial(gram_kernel, parts),
        out_shape=(half, half),
        in_specs=[pl.BlockSpec(memory_space=pltpu.SMEM)] + [pl.BlockSpec(memory_space=HBM)] * 2,
        out_specs=(pl.BlockSpec(memory_space=HBM),) * 2,
        scratch_shapes=[
            pltpu.VMEM((ROWS, WIDTH), BF16),
            pltpu.VMEM((WIDTH, ROWS), BF16),
            pltpu.VMEM((2, CHIPS, SLOTS, 8, 128), F32),
            pltpu.SemaphoreType.DMA((parts, 2)),
            pltpu.SemaphoreType.DMA((2,)),
        ],
        compiler_params=pltpu.CompilerParams(vmem_limit_bytes=48 * 2**20),
        cost_estimate=pl.CostEstimate(flops=2 * ROWS * WIDTH * WIDTH, bytes_accessed=10 * 2**20, transcendentals=0),
        name="gram",
    )(counts, patches, out_grads)


def collect_kernel(met, out):
    total = met[0]
    for n in range(1, CHIPS):
        total = total + met[n]
    out[...] = total


def collect(met):
    return pl.pallas_call(
        collect_kernel,
        out_shape=jax.ShapeDtypeStruct((SLOTS, 8, 128), F32),
        compiler_params=pltpu.CompilerParams(vmem_limit_bytes=16 * 2**20),
        name="collect",
    )(met)


def spread_kernel(done, twin, send, direct, total, flat):
    group, xl, core = position()
    own, other = done[...], twin[...]
    low = jnp.where(core == 0, own, other)
    high = jnp.where(core == 0, other, own)
    total[...] = jnp.broadcast_to(high[SLOTS - 1, 4:5], (8, 128))
    direct[...] = jnp.zeros_like(direct)
    shared = (9 * group + 4) // 16
    for v in range(4 * HALF + HALF // 2 + 1):
        here, slot = factor_slot(v)
        tile = high[slot] if here else low[slot]
        u, step = divmod(v, HALF)
        if u < 4:
            col = lax.rem((9 * group + 5 * xl + u) // 16 + step, BLOCKS)
            direct[col, 8 * u : 8 * u + 8, :] = tile
        else:
            direct[lax.rem(shared + 2 * step, BLOCKS), 32:36, :] = tile[0:4]
            if 2 * step + 1 < HALF:
                direct[lax.rem(shared + 2 * step + 1, BLOCKS), 32:36, :] = tile[4:8]
    pad = jnp.zeros((128 - 40, 128), F32)
    for col in range(BLOCKS):
        flat[0, 128 * col : 128 * col + 128, :] = jnp.concatenate([direct[col], pad], axis=0).T
    flat[0, DA : DA + 8, :] = jnp.zeros((8, 128), F32)
    for third in (1, 2):
        flat[third] = pltpu.roll(flat[0], 40 * third, 1)
    send[:, :GRADS] = jnp.broadcast_to(own[None, :GRADS], (CHIPS, GRADS, 8, 128))
    for here in (0, 1):

        @pl.when(core == here)
        def _():
            for n in range(CHIPS):
                first = 36 * n + 18 * here
                thirds = [flat[t, first + 6 * t : first + 6 * t + 8, :] for t in range(3)]
                send[n, GRADS] = thirds[0] + thirds[1] + thirds[2]


def spread(done, twin):
    vmem = pl.BlockSpec(memory_space=pltpu.VMEM)
    return pl.pallas_call(
        spread_kernel,
        out_shape=(
            jax.ShapeDtypeStruct((CHIPS, GRADS + 1, 8, 128), F32),
            jax.ShapeDtypeStruct((BLOCKS, 40, 128), F32),
            jax.ShapeDtypeStruct((8, 128), F32),
        ),
        in_specs=[vmem, vmem],
        out_specs=(vmem,) * 3,
        scratch_shapes=[pltpu.VMEM((3, DA + 8, 128), F32)],
        compiler_params=pltpu.CompilerParams(vmem_limit_bytes=16 * 2**20),
        name="spread",
    )(done, twin)


def rows_kernel(got, direct, total_ref, out, turned):
    group, xl, core = position()
    total = total_ref[0:1, 0:1]
    for n in range(CHIPS):
        for third in range(3):
            rows = slice(6 * third, 6 * third + 6)
            for to, first, size in ((4, 0, 32), (0, 32, 4)) if n % 2 else ((0, 0, 36),):
                first = first + 40 * third
                turned[rows, 36 * n + to : 36 * n + to + size] = got[n, GRADS, 0:6, first : first + size]
    start = 72 * group + 36 * xl + 18 * core
    block = (lax.broadcasted_iota(jnp.int32, (18, 128), 0) + start) // 128
    for here in range(4):

        @pl.when(2 * xl + core == here)
        def _():
            first = (0, 18, 0, 14)[here]
            for col in range(BLOCKS):
                step = col - block
                step = jnp.where(step < 0, step + BLOCKS, step)
                lanes = slice(128 * col, 128 * col + 128)
                if here == 2:
                    straight = jnp.concatenate([direct[col, 32:36, :], direct[col, 0:14, :]], axis=0)
                else:
                    straight = direct[col, first : first + 18, :]
                value = jnp.where(step < HALF, straight, turned[:18, lanes]) / total
                for i in range(18):
                    out[i, :, lanes] = value[i : i + 1, :]


def factor_rows(got, direct, total):
    vmem = pl.BlockSpec(memory_space=pltpu.VMEM)
    out = pl.pallas_call(
        rows_kernel,
        out_shape=jax.ShapeDtypeStruct((18, 1, DA), F32),
        in_specs=[vmem] * 3,
        scratch_shapes=[pltpu.VMEM((24, DA), F32)],
        compiler_params=pltpu.CompilerParams(vmem_limit_bytes=16 * 2**20),
        cost_estimate=pl.CostEstimate(flops=10**6, bytes_accessed=2**20, transcendentals=0),
        name="factor_rows",
    )(got, direct, total)
    return out.reshape(1, 18, DA)


def precond_kernel(got, other, total_ref, basis_a, basis_g, eig_a, eig_g, g_factor, precond):
    core = lax.axis_index("core")
    total = total_ref[0:1, 0:1]
    shape = (16, 2, GRADS + 1, 8, 128)
    both = (got[...].reshape(shape), other[...].reshape(shape))
    columns = []
    for col in range(WIDTH // 128):
        n, rest = divmod(col, 5)
        low, rest = (rest < 3), (rest if rest < 3 else rest - 3)
        tiles = jnp.where((core == 0) == low, both[0][:, n, rest], both[1][:, n, rest])
        columns.append(tiles.reshape(128, 128) / total)
    g_factor[0] = columns[-1]
    grad = jnp.concatenate([c.astype(BF16) for c in columns[:-1]], axis=1)
    left = lax.dot_general(basis_g[0], grad, (((0,), (0,)), ((), ())), preferred_element_type=F32).astype(BF16)
    rotated = jnp.dot(left, basis_a[0], preferred_element_type=F32)
    eig_rows = jnp.broadcast_to(eig_g[...], (DG, DG)).T[:, 0:1]
    scaled = (rotated / (eig_rows * eig_a[...] + 0.001)).astype(BF16)
    inner = jnp.dot(basis_g[0], scaled, preferred_element_type=F32).astype(BF16)
    precond[0] = lax.dot_general(inner, basis_a[0], (((1,), (1,)), ((), ())), preferred_element_type=F32)


def precondition(got, other, total, basis_a, basis_g, eig_a, eig_g):
    vmem = pl.BlockSpec(memory_space=pltpu.VMEM)
    return pl.pallas_call(
        precond_kernel,
        out_shape=(jax.ShapeDtypeStruct((1, DG, DG), F32), jax.ShapeDtypeStruct((1, DG, DA), F32)),
        in_specs=[vmem] * 7,
        compiler_params=pltpu.CompilerParams(vmem_limit_bytes=16 * 2**20),
        name="precondition",
    )(got, other, total, basis_a, basis_g, eig_a, eig_g)


def swap_cores(value):
    return lax.ppermute(value, "core", [(0, 1), (1, 0)])


def group_sum(value):
    for k in (1, 3):
        value = value + lax.ppermute(value, "zh", [(i, i ^ k) for i in range(4)])
    return value


def on_device(patches, out_grads, counts, basis_a, basis_g, eig_a, eig_g):
    mine, theirs = gram(patches, out_grads, counts)
    met = lax.all_to_all(mine + swap_cores(theirs), CHIP_AXES, 0, 0, tiled=True)
    done = group_sum(collect(met))
    send, direct, total = spread(done, swap_cores(done))
    got = lax.all_to_all(send, CHIP_AXES, 0, 0, tiled=True)
    other = swap_cores(got)
    a_factor = factor_rows(got, direct, total)
    g_factor, precond = precondition(got, other, total, basis_a, basis_g, eig_a, eig_g)
    return a_factor, g_factor, precond


def solution(mesh):
    axes = ("zl", "y", "xh", "xl", "core", "zh")
    finer = Mesh(mesh.devices.reshape(2, 4, 2, 2, 2, 4), axes)
    placed = (P(None, axes, None), P(None, axes, None), P(axes), P(), P(), P(), P())
    return jax.shard_map(
        on_device,
        mesh=finer,
        in_specs=placed,
        out_specs=(P(None, axes[:-1], None), P(), P()),
        check_vma=False,
    )
```

```python
import jax
import jax.numpy as jnp
from jax import lax
from jax.experimental import pallas as pl
from jax.experimental.pallas import tpu as pltpu
from jax.sharding import Mesh, PartitionSpec as P

DA, DG, ROWS = 1152, 128, 2048
WIDTH = DA + DG
PARTS = (0, 512, ROWS)
BLOCKS = DA // 128
HALF = BLOCKS // 2 + 1
CHIPS, SLOTS, GRADS = 32, 14, 3
LOW = SLOTS - GRADS
CHIP_AXES = ("zl", "y", "xh", "xl")
HBM = pltpu.MemorySpace.HBM
F32, BF16 = jnp.float32, jnp.bfloat16


def factor_slot(v):
    return (0, GRADS + v) if v < LOW else (1, GRADS - 1 + v - LOW)


def factor_places(row8, step):
    group, within = divmod(row8, 9)
    if within == 4:
        core, slot = factor_slot(4 * HALF + step // 2)
        to = slice(4 * (step % 2), 4 * (step % 2) + 4)
        for xl in (0, 1):
            yield (core, 2 * group + xl, slot, to), slice(4 * xl, 4 * xl + 4)
    else:
        xl = within // 5
        core, slot = factor_slot((within - 5 * xl) * HALF + step)
        yield (core, 2 * group + xl, slot, slice(0, 8)), slice(0, 8)


def grad_place(row8, col):
    chip, rest = divmod(row8 * 10 + col, 5)
    return (0, chip, rest, slice(0, 8)) if rest < 3 else (1, chip, rest - 3, slice(0, 8))


def position():
    group = (lax.axis_index("zl") * 4 + lax.axis_index("y")) * 2 + lax.axis_index("xh")
    return group, lax.axis_index("xl"), lax.axis_index("core")


def products(part, z, zt, acc):
    depth = slice(PARTS[part], PARTS[part + 1])

    def put(place, tile):
        acc[place] = acc[place] + tile if part else tile

    for col0 in range(0, BLOCKS + 1, 2):
        wanted = sorted({(c - s) % BLOCKS for c in (col0, col0 + 1) if c < BLOCKS for s in range(HALF)}) + [BLOCKS]
        runs = []
        for i in wanted:
            if runs and runs[-1][-1] == i - 1:
                runs[-1].append(i)
            else:
                runs.append([i])
        for run in runs:
            w = jnp.dot(
                zt[128 * run[0] : 128 * run[-1] + 128, depth],
                z[depth, 128 * col0 : 128 * col0 + 256],
                preferred_element_type=F32,
            )
            for u in range(16 * len(run)):
                row8 = 16 * run[0] + u
                for v in (0, 1):
                    tile = w[8 * u : 8 * u + 8, 128 * v : 128 * v + 128]
                    if row8 >= DA // 8:
                        put(grad_place(row8 - DA // 8, col0 + v), tile)
                    elif col0 + v < BLOCKS and (col0 + v - row8 // 16) % BLOCKS < HALF:
                        for place, rows in factor_places(row8, (col0 + v - row8 // 16) % BLOCKS):
                            put(place, tile[rows])


def gram_kernel(count_ref, x_hbm, y_hbm, mine, theirs, z, zt, acc, in_sem, out_sem):
    copies = []
    for k in range(len(PARTS) - 1):
        rows = pl.ds(PARTS[k], PARTS[k + 1] - PARTS[k])
        copies.append(
            (
                pltpu.make_async_copy(x_hbm.at[0, rows, :], z.at[rows, pl.ds(0, DA)], in_sem.at[k, 0]),
                pltpu.make_async_copy(y_hbm.at[0, rows, :], z.at[rows, pl.ds(DA, DG)], in_sem.at[k, 1]),
            )
        )
        for copy in copies[k]:
            copy.start()
    count, core = count_ref[0], lax.axis_index("core")
    acc[1, :, SLOTS - 1, 4:8, :] = jnp.full((CHIPS, 4, 128), count.astype(F32))
    for k in range(len(PARTS) - 1):
        for copy in copies[k]:
            copy.wait()
        here = slice(PARTS[k], PARTS[k + 1])
        row = lax.broadcasted_iota(jnp.int32, (PARTS[k + 1] - PARTS[k], 1), 0) + PARTS[k]
        zt[:, here] = jnp.where(row < count, z[here, :], jnp.zeros((), BF16)).T
        products(k, z, zt, acc)
    first = pltpu.make_async_copy(acc.at[1 - core], theirs, out_sem.at[0])
    second = pltpu.make_async_copy(acc.at[core], mine, out_sem.at[1])
    first.start()
    second.start()
    first.wait()
    second.wait()


def gram(patches, out_grads, counts):
    half = jax.ShapeDtypeStruct((CHIPS, SLOTS, 8, 128), F32)
    return pl.pallas_call(
        gram_kernel,
        out_shape=(half, half),
        in_specs=[pl.BlockSpec(memory_space=pltpu.SMEM)] + [pl.BlockSpec(memory_space=HBM)] * 2,
        out_specs=(pl.BlockSpec(memory_space=HBM),) * 2,
        scratch_shapes=[
            pltpu.VMEM((ROWS, WIDTH), BF16),
            pltpu.VMEM((WIDTH, ROWS), BF16),
            pltpu.VMEM((2, CHIPS, SLOTS, 8, 128), F32),
            pltpu.SemaphoreType.DMA((len(PARTS) - 1, 2)),
            pltpu.SemaphoreType.DMA((2,)),
        ],
        compiler_params=pltpu.CompilerParams(vmem_limit_bytes=48 * 2**20),
        cost_estimate=pl.CostEstimate(flops=2 * ROWS * WIDTH * WIDTH, bytes_accessed=10 * 2**20, transcendentals=0),
        name="gram",
    )(counts, patches, out_grads)


def collect_kernel(met, out):
    total = met[0]
    for n in range(1, CHIPS):
        total = total + met[n]
    out[...] = total


def collect(met):
    return pl.pallas_call(
        collect_kernel,
        out_shape=jax.ShapeDtypeStruct((SLOTS, 8, 128), F32),
        compiler_params=pltpu.CompilerParams(vmem_limit_bytes=16 * 2**20),
        name="collect",
    )(met)


def spread_kernel(done, twin, send, direct, total, flat):
    group, xl, core = position()
    own, other = done[...], twin[...]
    low = jnp.where(core == 0, own, other)
    high = jnp.where(core == 0, other, own)
    total[...] = jnp.broadcast_to(high[SLOTS - 1, 4:5], (8, 128))
    direct[...] = jnp.zeros_like(direct)
    shared = (9 * group + 4) // 16
    for v in range(4 * HALF + HALF // 2 + 1):
        here, slot = factor_slot(v)
        tile = high[slot] if here else low[slot]
        u, step = divmod(v, HALF)
        if u < 4:
            col = lax.rem((9 * group + 5 * xl + u) // 16 + step, BLOCKS)
            direct[col, 8 * u : 8 * u + 8, :] = tile
        else:
            direct[lax.rem(shared + 2 * step, BLOCKS), 32:36, :] = tile[0:4]
            if 2 * step + 1 < HALF:
                direct[lax.rem(shared + 2 * step + 1, BLOCKS), 32:36, :] = tile[4:8]
    pad = jnp.zeros((128 - 40, 128), F32)
    for col in range(BLOCKS):
        flat[0, 128 * col : 128 * col + 128, :] = jnp.concatenate([direct[col], pad], axis=0).T
    flat[0, DA : DA + 8, :] = jnp.zeros((8, 128), F32)
    for third in (1, 2):
        flat[third] = pltpu.roll(flat[0], 40 * third, 1)
    send[:, :GRADS] = jnp.broadcast_to(own[None, :GRADS], (CHIPS, GRADS, 8, 128))
    for here in (0, 1):

        @pl.when(core == here)
        def _():
            for n in range(CHIPS):
                first = 36 * n + 18 * here
                thirds = [flat[t, first + 6 * t : first + 6 * t + 8, :] for t in range(3)]
                send[n, GRADS] = thirds[0] + thirds[1] + thirds[2]


def spread(done, twin):
    vmem = pl.BlockSpec(memory_space=pltpu.VMEM)
    return pl.pallas_call(
        spread_kernel,
        out_shape=(
            jax.ShapeDtypeStruct((CHIPS, GRADS + 1, 8, 128), F32),
            jax.ShapeDtypeStruct((BLOCKS, 40, 128), F32),
            jax.ShapeDtypeStruct((8, 128), F32),
        ),
        in_specs=[vmem, vmem],
        out_specs=(vmem,) * 3,
        scratch_shapes=[pltpu.VMEM((3, DA + 8, 128), F32)],
        compiler_params=pltpu.CompilerParams(vmem_limit_bytes=16 * 2**20),
        name="spread",
    )(done, twin)


def rows_kernel(got, direct, total_ref, out, turned):
    group, xl, core = position()
    total = total_ref[0:1, 0:1]
    for n in range(CHIPS):
        for third in range(3):
            rows = slice(6 * third, 6 * third + 6)
            for to, first, size in ((4, 0, 32), (0, 32, 4)) if n % 2 else ((0, 0, 36),):
                first = first + 40 * third
                turned[rows, 36 * n + to : 36 * n + to + size] = got[n, GRADS, 0:6, first : first + size]
    start = 72 * group + 36 * xl + 18 * core
    block = (lax.broadcasted_iota(jnp.int32, (18, 128), 0) + start) // 128
    for here in range(4):

        @pl.when(2 * xl + core == here)
        def _():
            first = (0, 18, 0, 14)[here]
            for col in range(BLOCKS):
                step = col - block
                step = jnp.where(step < 0, step + BLOCKS, step)
                lanes = slice(128 * col, 128 * col + 128)
                if here == 2:
                    straight = jnp.concatenate([direct[col, 32:36, :], direct[col, 0:14, :]], axis=0)
                else:
                    straight = direct[col, first : first + 18, :]
                value = jnp.where(step < HALF, straight, turned[:18, lanes]) / total
                for i in range(18):
                    out[i, :, lanes] = value[i : i + 1, :]


def factor_rows(got, direct, total):
    vmem = pl.BlockSpec(memory_space=pltpu.VMEM)
    out = pl.pallas_call(
        rows_kernel,
        out_shape=jax.ShapeDtypeStruct((18, 1, DA), F32),
        in_specs=[vmem] * 3,
        scratch_shapes=[pltpu.VMEM((24, DA), F32)],
        compiler_params=pltpu.CompilerParams(vmem_limit_bytes=16 * 2**20),
        cost_estimate=pl.CostEstimate(flops=10**6, bytes_accessed=2**20, transcendentals=0),
        name="factor_rows",
    )(got, direct, total)
    return out.reshape(1, 18, DA)


def precond_kernel(got, other, total_ref, basis_a, basis_g, eig_a, eig_g, g_factor, precond):
    core = lax.axis_index("core")
    total = total_ref[0:1, 0:1]
    shape = (16, 2, GRADS + 1, 8, 128)
    both = (got[...].reshape(shape), other[...].reshape(shape))
    columns = []
    for col in range(WIDTH // 128):
        n, rest = divmod(col, 5)
        low, rest = (rest < 3), (rest if rest < 3 else rest - 3)
        tiles = jnp.where((core == 0) == low, both[0][:, n, rest], both[1][:, n, rest])
        columns.append(tiles.reshape(128, 128) / total)
    g_factor[0] = columns[-1]
    grad = jnp.concatenate([c.astype(BF16) for c in columns[:-1]], axis=1)
    left = lax.dot_general(basis_g[0], grad, (((0,), (0,)), ((), ())), preferred_element_type=F32).astype(BF16)
    rotated = jnp.dot(left, basis_a[0], preferred_element_type=F32)
    eig_rows = jnp.broadcast_to(eig_g[...], (DG, DG)).T[:, 0:1]
    scaled = (rotated / (eig_rows * eig_a[...] + 0.001)).astype(BF16)
    inner = jnp.dot(basis_g[0], scaled, preferred_element_type=F32).astype(BF16)
    precond[0] = lax.dot_general(inner, basis_a[0], (((1,), (1,)), ((), ())), preferred_element_type=F32)


def precondition(got, other, total, basis_a, basis_g, eig_a, eig_g):
    vmem = pl.BlockSpec(memory_space=pltpu.VMEM)
    return pl.pallas_call(
        precond_kernel,
        out_shape=(jax.ShapeDtypeStruct((1, DG, DG), F32), jax.ShapeDtypeStruct((1, DG, DA), F32)),
        in_specs=[vmem] * 7,
        compiler_params=pltpu.CompilerParams(vmem_limit_bytes=16 * 2**20),
        name="precondition",
    )(got, other, total, basis_a, basis_g, eig_a, eig_g)


def swap_cores(value):
    return lax.ppermute(value, "core", [(0, 1), (1, 0)])


def group_sums(value):
    value = value + lax.ppermute(value, "zh", [(i, i ^ 1) for i in range(4)])
    far = lax.ppermute(value, "zh", [(i, i ^ 3) for i in range(4)])
    twin = swap_cores(value)
    twin_far = lax.ppermute(value, ("core", "zh"), [(i, i ^ 7) for i in range(8)])
    return value + far, twin + twin_far


def on_device(patches, out_grads, counts, basis_a, basis_g, eig_a, eig_g):
    mine, theirs = gram(patches, out_grads, counts)
    met = lax.all_to_all(mine + swap_cores(theirs), CHIP_AXES, 0, 0, tiled=True)
    send, direct, total = spread(*group_sums(collect(met)))
    got = lax.all_to_all(send, CHIP_AXES, 0, 0, tiled=True)
    other = swap_cores(got)
    a_factor = factor_rows(got, direct, total)
    g_factor, precond = precondition(got, other, total, basis_a, basis_g, eig_a, eig_g)
    return a_factor, g_factor, precond


def solution(mesh):
    axes = ("zl", "y", "xh", "xl", "core", "zh")
    finer = Mesh(mesh.devices.reshape(2, 4, 2, 2, 2, 4), axes)
    placed = (P(None, axes, None), P(None, axes, None), P(axes), P(), P(), P(), P())
    return jax.shard_map(
        on_device,
        mesh=finer,
        in_specs=placed,
        out_specs=(P(None, axes[:-1], None), P(), P()),
        check_vma=False,
    )
```

```python
import jax
import jax.numpy as jnp
from jax import lax
from jax.experimental import pallas as pl
from jax.experimental.pallas import tpu as pltpu
from jax.sharding import PartitionSpec as P

DA, DG, ROWS = 1152, 128, 2048
WIDTH = DA + DG
PARTS = (0, 512, ROWS)
BLOCKS = DA // 128
HALF = BLOCKS // 2 + 1
CHIPS, SLOTS, GRADS = 32, 14, 3
LOW = SLOTS - GRADS
CHIP_GROUPS = [[2 * n + core for n in range(CHIPS)] for core in (0, 1)]
FIRST = [[32 * zl + 8 * y + 2 * x for x in range(4)] for zl in range(2) for y in range(4)]
FIRST += [[32 * zl + 8 * y + 2 * x + 1 for y in range(4)] for zl in range(2) for x in range(4)]
SECOND = [[32 * zl + 8 * y + 2 * x for zl in range(2) for y in range(4)] for x in range(4)]
SECOND += [[32 * zl + 8 * y + 2 * x + 1 for zl in range(2) for x in range(4)] for y in range(4)]
HBM = pltpu.MemorySpace.HBM
F32, BF16 = jnp.float32, jnp.bfloat16


def factor_slot(v):
    return (0, GRADS + v) if v < LOW else (1, GRADS - 1 + v - LOW)


def factor_places(row8, step):
    group, within = divmod(row8, 9)
    if within == 4:
        core, slot = factor_slot(4 * HALF + step // 2)
        to = slice(4 * (step % 2), 4 * (step % 2) + 4)
        for xl in (0, 1):
            yield (core, 2 * group + xl, slot, to), slice(4 * xl, 4 * xl + 4)
    else:
        xl = within // 5
        core, slot = factor_slot((within - 5 * xl) * HALF + step)
        yield (core, 2 * group + xl, slot, slice(0, 8)), slice(0, 8)


def grad_place(row8, col):
    chip, rest = divmod(row8 * 10 + col, 5)
    return (0, chip, rest, slice(0, 8)) if rest < 3 else (1, chip, rest - 3, slice(0, 8))


def position():
    dp = lax.axis_index("dp")
    return lax.div(dp, 4), lax.rem(lax.div(dp, 2), 2), lax.rem(dp, 2)


def ordered(core, chip):
    zl, y, x = chip // 16, chip // 4 % 4, chip % 4
    return (y, 4 * zl + x) if core else (x, 4 * zl + y)


def products(part, z, zt, acc):
    depth = slice(PARTS[part], PARTS[part + 1])

    def put(place, tile):
        place = place[:1] + ordered(*place[:2]) + place[2:]
        acc[place] = acc[place] + tile if part else tile

    for col0 in range(0, BLOCKS + 1, 2):
        wanted = sorted({(c - s) % BLOCKS for c in (col0, col0 + 1) if c < BLOCKS for s in range(HALF)}) + [BLOCKS]
        runs = []
        for i in wanted:
            if runs and runs[-1][-1] == i - 1:
                runs[-1].append(i)
            else:
                runs.append([i])
        for run in runs:
            w = jnp.dot(
                zt[128 * run[0] : 128 * run[-1] + 128, depth],
                z[depth, 128 * col0 : 128 * col0 + 256],
                preferred_element_type=F32,
            )
            for u in range(16 * len(run)):
                row8 = 16 * run[0] + u
                for v in (0, 1):
                    tile = w[8 * u : 8 * u + 8, 128 * v : 128 * v + 128]
                    if row8 >= DA // 8:
                        put(grad_place(row8 - DA // 8, col0 + v), tile)
                    elif col0 + v < BLOCKS and (col0 + v - row8 // 16) % BLOCKS < HALF:
                        for place, rows in factor_places(row8, (col0 + v - row8 // 16) % BLOCKS):
                            put(place, tile[rows])


def gram_kernel(count_ref, x_hbm, y_hbm, mine, theirs, z, zt, acc, in_sem, out_sem):
    copies = []
    for k in range(len(PARTS) - 1):
        rows = pl.ds(PARTS[k], PARTS[k + 1] - PARTS[k])
        copies.append(
            (
                pltpu.make_async_copy(x_hbm.at[0, rows, :], z.at[rows, pl.ds(0, DA)], in_sem.at[k, 0]),
                pltpu.make_async_copy(y_hbm.at[0, rows, :], z.at[rows, pl.ds(DA, DG)], in_sem.at[k, 1]),
            )
        )
        for copy in copies[k]:
            copy.start()
    count, core = count_ref[0], lax.rem(lax.axis_index("dp"), 2)
    acc[1, :, :, SLOTS - 1, 4:8, :] = jnp.full((4, 8, 4, 128), count.astype(F32))
    for k in range(len(PARTS) - 1):
        for copy in copies[k]:
            copy.wait()
        here = slice(PARTS[k], PARTS[k + 1])
        row = lax.broadcasted_iota(jnp.int32, (PARTS[k + 1] - PARTS[k], 1), 0) + PARTS[k]
        zt[:, here] = jnp.where(row < count, z[here, :], jnp.zeros((), BF16)).T
        products(k, z, zt, acc)
    first = pltpu.make_async_copy(acc.at[1 - core], theirs, out_sem.at[0])
    second = pltpu.make_async_copy(acc.at[core], mine, out_sem.at[1])
    first.start()
    second.start()
    first.wait()
    second.wait()


def gram(patches, out_grads, counts):
    half = jax.ShapeDtypeStruct((4, 8, SLOTS, 8, 128), F32)
    return pl.pallas_call(
        gram_kernel,
        out_shape=(half, half),
        in_specs=[pl.BlockSpec(memory_space=pltpu.SMEM)] + [pl.BlockSpec(memory_space=HBM)] * 2,
        out_specs=(pl.BlockSpec(memory_space=HBM),) * 2,
        scratch_shapes=[
            pltpu.VMEM((ROWS, WIDTH), BF16),
            pltpu.VMEM((WIDTH, ROWS), BF16),
            pltpu.VMEM((2, 4, 8, SLOTS, 8, 128), F32),
            pltpu.SemaphoreType.DMA((len(PARTS) - 1, 2)),
            pltpu.SemaphoreType.DMA((2,)),
        ],
        compiler_params=pltpu.CompilerParams(vmem_limit_bytes=48 * 2**20),
        cost_estimate=pl.CostEstimate(flops=2 * ROWS * WIDTH * WIDTH, bytes_accessed=10 * 2**20, transcendentals=0),
        name="gram",
    )(counts, patches, out_grads)


def collect_kernel(met, out):
    total = met[0]
    for n in range(1, met.shape[0]):
        total = total + met[n]
    out[...] = total


def collect(met):
    return pl.pallas_call(
        collect_kernel,
        out_shape=jax.ShapeDtypeStruct(met.shape[1:], F32),
        compiler_params=pltpu.CompilerParams(vmem_limit_bytes=16 * 2**20),
        name="collect",
    )(met)


def spread_kernel(done, twin, send, direct, total, flat):
    group, xl, core = position()
    own, other = done[...], twin[...]
    low = jnp.where(core == 0, own, other)
    high = jnp.where(core == 0, other, own)
    total[...] = jnp.broadcast_to(high[SLOTS - 1, 4:5], (8, 128))
    direct[...] = jnp.zeros_like(direct)
    shared = (9 * group + 4) // 16
    for v in range(4 * HALF + HALF // 2 + 1):
        here, slot = factor_slot(v)
        tile = high[slot] if here else low[slot]
        u, step = divmod(v, HALF)
        if u < 4:
            col = lax.rem((9 * group + 5 * xl + u) // 16 + step, BLOCKS)
            direct[col, 8 * u : 8 * u + 8, :] = tile
        else:
            direct[lax.rem(shared + 2 * step, BLOCKS), 32:36, :] = tile[0:4]
            if 2 * step + 1 < HALF:
                direct[lax.rem(shared + 2 * step + 1, BLOCKS), 32:36, :] = tile[4:8]
    pad = jnp.zeros((128 - 40, 128), F32)
    for col in range(BLOCKS):
        flat[0, 128 * col : 128 * col + 128, :] = jnp.concatenate([direct[col], pad], axis=0).T
    flat[0, DA : DA + 8, :] = jnp.zeros((8, 128), F32)
    for third in (1, 2):
        flat[third] = pltpu.roll(flat[0], 40 * third, 1)
    send[:, :GRADS] = jnp.broadcast_to(own[None, :GRADS], (CHIPS, GRADS, 8, 128))
    for here in (0, 1):

        @pl.when(core == here)
        def _():
            for n in range(CHIPS):
                first = 36 * n + 18 * here
                thirds = [flat[t, first + 6 * t : first + 6 * t + 8, :] for t in range(3)]
                send[n, GRADS] = thirds[0] + thirds[1] + thirds[2]


def spread(done, twin):
    vmem = pl.BlockSpec(memory_space=pltpu.VMEM)
    return pl.pallas_call(
        spread_kernel,
        out_shape=(
            jax.ShapeDtypeStruct((CHIPS, GRADS + 1, 8, 128), F32),
            jax.ShapeDtypeStruct((BLOCKS, 40, 128), F32),
            jax.ShapeDtypeStruct((8, 128), F32),
        ),
        in_specs=[vmem, vmem],
        out_specs=(vmem,) * 3,
        scratch_shapes=[pltpu.VMEM((3, DA + 8, 128), F32)],
        compiler_params=pltpu.CompilerParams(vmem_limit_bytes=16 * 2**20),
        name="spread",
    )(done, twin)


def rows_kernel(got, direct, total_ref, out, turned):
    group, xl, core = position()
    total = total_ref[0:1, 0:1]
    for n in range(CHIPS):
        for third in range(3):
            rows = slice(6 * third, 6 * third + 6)
            for to, first, size in ((4, 0, 32), (0, 32, 4)) if n % 2 else ((0, 0, 36),):
                first = first + 40 * third
                turned[rows, 36 * n + to : 36 * n + to + size] = got[n, GRADS, 0:6, first : first + size]
    start = 72 * group + 36 * xl + 18 * core
    block = (lax.broadcasted_iota(jnp.int32, (18, 128), 0) + start) // 128
    for here in range(4):

        @pl.when(2 * xl + core == here)
        def _():
            first = (0, 18, 0, 14)[here]
            for col in range(BLOCKS):
                step = col - block
                step = jnp.where(step < 0, step + BLOCKS, step)
                lanes = slice(128 * col, 128 * col + 128)
                if here == 2:
                    straight = jnp.concatenate([direct[col, 32:36, :], direct[col, 0:14, :]], axis=0)
                else:
                    straight = direct[col, first : first + 18, :]
                value = jnp.where(step < HALF, straight, turned[:18, lanes]) / total
                for i in range(18):
                    out[i, :, lanes] = value[i : i + 1, :]


def factor_rows(got, direct, total):
    vmem = pl.BlockSpec(memory_space=pltpu.VMEM)
    out = pl.pallas_call(
        rows_kernel,
        out_shape=jax.ShapeDtypeStruct((18, 1, DA), F32),
        in_specs=[vmem] * 3,
        scratch_shapes=[pltpu.VMEM((24, DA), F32)],
        compiler_params=pltpu.CompilerParams(vmem_limit_bytes=16 * 2**20),
        cost_estimate=pl.CostEstimate(flops=10**6, bytes_accessed=2**20, transcendentals=0),
        name="factor_rows",
    )(got, direct, total)
    return out.reshape(1, 18, DA)


def precond_kernel(got, other, total_ref, basis_a, basis_g, eig_a, eig_g, g_factor, precond):
    core = lax.rem(lax.axis_index("dp"), 2)
    total = total_ref[0:1, 0:1]
    shape = (16, 2, GRADS + 1, 8, 128)
    both = (got[...].reshape(shape), other[...].reshape(shape))
    columns = []
    for col in range(WIDTH // 128):
        n, rest = divmod(col, 5)
        low, rest = (rest < 3), (rest if rest < 3 else rest - 3)
        tiles = jnp.where((core == 0) == low, both[0][:, n, rest], both[1][:, n, rest])
        columns.append(tiles.reshape(128, 128) / total)
    g_factor[0] = columns[-1]
    grad = jnp.concatenate([c.astype(BF16) for c in columns[:-1]], axis=1)
    left = lax.dot_general(basis_g[0], grad, (((0,), (0,)), ((), ())), preferred_element_type=F32).astype(BF16)
    rotated = jnp.dot(left, basis_a[0], preferred_element_type=F32)
    eig_rows = jnp.broadcast_to(eig_g[...], (DG, DG)).T[:, 0:1]
    scaled = (rotated / (eig_rows * eig_a[...] + 0.001)).astype(BF16)
    inner = jnp.dot(basis_g[0], scaled, preferred_element_type=F32).astype(BF16)
    precond[0] = lax.dot_general(inner, basis_a[0], (((1,), (1,)), ((), ())), preferred_element_type=F32)


def precondition(got, other, total, basis_a, basis_g, eig_a, eig_g):
    vmem = pl.BlockSpec(memory_space=pltpu.VMEM)
    return pl.pallas_call(
        precond_kernel,
        out_shape=(jax.ShapeDtypeStruct((1, DG, DG), F32), jax.ShapeDtypeStruct((1, DG, DA), F32)),
        in_specs=[vmem] * 7,
        compiler_params=pltpu.CompilerParams(vmem_limit_bytes=16 * 2**20),
        name="precondition",
    )(got, other, total, basis_a, basis_g, eig_a, eig_g)


def swap_cores(value):
    return lax.ppermute(value, "dp", [(i, i ^ 1) for i in range(64)])


def group_sums(value):
    value = value + lax.ppermute(value, "grp", [(i, i ^ 1) for i in range(4)])
    far = lax.ppermute(value, "grp", [(i, i ^ 3) for i in range(4)])
    twin = swap_cores(value)
    twin_far = lax.ppermute(value, ("dp", "grp"), [(i, i ^ 7) for i in range(256)])
    return value + far, twin + twin_far


def exchange(value, groups):
    return lax.all_to_all(value, "dp", 0, 0, axis_index_groups=groups, tiled=True)


def on_device(patches, out_grads, counts, basis_a, basis_g, eig_a, eig_g):
    mine, theirs = gram(patches, out_grads, counts)
    line = collect(exchange(mine + swap_cores(theirs), FIRST))
    part = collect(exchange(line, SECOND))
    send, direct, total = spread(*group_sums(part))
    got = exchange(send, CHIP_GROUPS)
    other = swap_cores(got)
    a_factor = factor_rows(got, direct, total)
    g_factor, precond = precondition(got, other, total, basis_a, basis_g, eig_a, eig_g)
    return a_factor, g_factor, precond


def solution(mesh):
    both = ("dp", "grp")
    placed = (P(None, both, None), P(None, both, None), P(both), P(), P(), P(), P())
    return jax.shard_map(
        on_device,
        mesh=mesh,
        in_specs=placed,
        out_specs=(P(None, "dp", None), P(), P()),
        check_vma=False,
    )
```

```python
import jax
import jax.numpy as jnp
from jax import lax
from jax.experimental import pallas as pl
from jax.experimental.pallas import tpu as pltpu
from jax.sharding import PartitionSpec as P

DA, DG, ROWS = 1152, 128, 2048
WIDTH = DA + DG
PARTS = (0, 512, ROWS)
BLOCKS = DA // 128
HALF = BLOCKS // 2 + 1
CHIPS, SLOTS, GRADS = 32, 14, 3
LOW = SLOTS - GRADS


def device(kind, zl, y, x):
    return 32 * zl + 8 * y + 2 * x + (kind + x + y) % 2


CHIP_GROUPS = [[device(kind, n // 16, n // 4 % 4, n % 4) for n in range(CHIPS)] for kind in (0, 1)]
FIRST = [[device(0, zl, y, x) for x in range(4)] for zl in range(2) for y in range(4)]
FIRST += [[device(1, zl, y, x) for y in range(4)] for zl in range(2) for x in range(4)]
SECOND = [[device(0, zl, y, x) for zl in range(2) for y in range(4)] for x in range(4)]
SECOND += [[device(1, zl, y, x) for zl in range(2) for x in range(4)] for y in range(4)]
HBM = pltpu.MemorySpace.HBM
F32, BF16 = jnp.float32, jnp.bfloat16


def factor_slot(v):
    return (0, GRADS + v) if v < LOW else (1, GRADS - 1 + v - LOW)


def factor_places(row8, step):
    group, within = divmod(row8, 9)
    if within == 4:
        core, slot = factor_slot(4 * HALF + step // 2)
        to = slice(4 * (step % 2), 4 * (step % 2) + 4)
        for xl in (0, 1):
            yield (core, 2 * group + xl, slot, to), slice(4 * xl, 4 * xl + 4)
    else:
        xl = within // 5
        core, slot = factor_slot((within - 5 * xl) * HALF + step)
        yield (core, 2 * group + xl, slot, slice(0, 8)), slice(0, 8)


def grad_place(row8, col):
    chip, rest = divmod(row8 * 10 + col, 5)
    return (0, chip, rest, slice(0, 8)) if rest < 3 else (1, chip, rest - 3, slice(0, 8))


def position():
    dp = lax.axis_index("dp")
    x, y, core = lax.rem(lax.div(dp, 2), 4), lax.rem(lax.div(dp, 8), 4), lax.rem(dp, 2)
    return lax.div(dp, 4), lax.rem(x, 2), core, lax.rem(core + x + y, 2)


def ordered(kind, chip):
    zl, y, x = chip // 16, chip // 4 % 4, chip % 4
    return (y, 4 * zl + x) if kind else (x, 4 * zl + y)


def products(part, z, zt, acc):
    depth = slice(PARTS[part], PARTS[part + 1])

    def put(place, tile):
        place = place[:1] + ordered(*place[:2]) + place[2:]
        acc[place] = acc[place] + tile if part else tile

    for col0 in range(0, BLOCKS + 1, 2):
        wanted = sorted({(c - s) % BLOCKS for c in (col0, col0 + 1) if c < BLOCKS for s in range(HALF)}) + [BLOCKS]
        runs = []
        for i in wanted:
            if runs and runs[-1][-1] == i - 1:
                runs[-1].append(i)
            else:
                runs.append([i])
        for run in runs:
            w = jnp.dot(
                zt[128 * run[0] : 128 * run[-1] + 128, depth],
                z[depth, 128 * col0 : 128 * col0 + 256],
                preferred_element_type=F32,
            )
            for u in range(16 * len(run)):
                row8 = 16 * run[0] + u
                for v in (0, 1):
                    tile = w[8 * u : 8 * u + 8, 128 * v : 128 * v + 128]
                    if row8 >= DA // 8:
                        put(grad_place(row8 - DA // 8, col0 + v), tile)
                    elif col0 + v < BLOCKS and (col0 + v - row8 // 16) % BLOCKS < HALF:
                        for place, rows in factor_places(row8, (col0 + v - row8 // 16) % BLOCKS):
                            put(place, tile[rows])


def gram_kernel(count_ref, x_hbm, y_hbm, mine, theirs, z, zt, acc, in_sem, out_sem):
    copies = []
    for k in range(len(PARTS) - 1):
        rows = pl.ds(PARTS[k], PARTS[k + 1] - PARTS[k])
        copies.append(
            (
                pltpu.make_async_copy(x_hbm.at[0, rows, :], z.at[rows, pl.ds(0, DA)], in_sem.at[k, 0]),
                pltpu.make_async_copy(y_hbm.at[0, rows, :], z.at[rows, pl.ds(DA, DG)], in_sem.at[k, 1]),
            )
        )
        for copy in copies[k]:
            copy.start()
    count, kind = count_ref[0], position()[3]
    acc[1, :, :, SLOTS - 1, 4:8, :] = jnp.full((4, 8, 4, 128), count.astype(F32))
    for k in range(len(PARTS) - 1):
        for copy in copies[k]:
            copy.wait()
        here = slice(PARTS[k], PARTS[k + 1])
        row = lax.broadcasted_iota(jnp.int32, (PARTS[k + 1] - PARTS[k], 1), 0) + PARTS[k]
        zt[:, here] = jnp.where(row < count, z[here, :], jnp.zeros((), BF16)).T
        products(k, z, zt, acc)
    first = pltpu.make_async_copy(acc.at[1 - kind], theirs, out_sem.at[0])
    second = pltpu.make_async_copy(acc.at[kind], mine, out_sem.at[1])
    first.start()
    second.start()
    first.wait()
    second.wait()


def gram(patches, out_grads, counts):
    half = jax.ShapeDtypeStruct((4, 8, SLOTS, 8, 128), F32)
    return pl.pallas_call(
        gram_kernel,
        out_shape=(half, half),
        in_specs=[pl.BlockSpec(memory_space=pltpu.SMEM)] + [pl.BlockSpec(memory_space=HBM)] * 2,
        out_specs=(pl.BlockSpec(memory_space=HBM),) * 2,
        scratch_shapes=[
            pltpu.VMEM((ROWS, WIDTH), BF16),
            pltpu.VMEM((WIDTH, ROWS), BF16),
            pltpu.VMEM((2, 4, 8, SLOTS, 8, 128), F32),
            pltpu.SemaphoreType.DMA((len(PARTS) - 1, 2)),
            pltpu.SemaphoreType.DMA((2,)),
        ],
        compiler_params=pltpu.CompilerParams(vmem_limit_bytes=48 * 2**20),
        cost_estimate=pl.CostEstimate(flops=2 * ROWS * WIDTH * WIDTH, bytes_accessed=10 * 2**20, transcendentals=0),
        name="gram",
    )(counts, patches, out_grads)


def collect_kernel(met, out):
    total = met[0]
    for n in range(1, met.shape[0]):
        total = total + met[n]
    out[...] = total


def collect(met):
    return pl.pallas_call(
        collect_kernel,
        out_shape=jax.ShapeDtypeStruct(met.shape[1:], F32),
        compiler_params=pltpu.CompilerParams(vmem_limit_bytes=16 * 2**20),
        name="collect",
    )(met)


def spread_kernel(done, twin, send, direct, total, flat):
    group, xl, _, kind = position()
    own, other = done[...], twin[...]
    low = jnp.where(kind == 0, own, other)
    high = jnp.where(kind == 0, other, own)
    total[...] = jnp.broadcast_to(high[SLOTS - 1, 4:5], (8, 128))
    direct[...] = jnp.zeros_like(direct)
    shared = (9 * group + 4) // 16
    for v in range(4 * HALF + HALF // 2 + 1):
        here, slot = factor_slot(v)
        tile = high[slot] if here else low[slot]
        u, step = divmod(v, HALF)
        if u < 4:
            col = lax.rem((9 * group + 5 * xl + u) // 16 + step, BLOCKS)
            direct[col, 8 * u : 8 * u + 8, :] = tile
        else:
            direct[lax.rem(shared + 2 * step, BLOCKS), 32:36, :] = tile[0:4]
            if 2 * step + 1 < HALF:
                direct[lax.rem(shared + 2 * step + 1, BLOCKS), 32:36, :] = tile[4:8]
    pad = jnp.zeros((128 - 40, 128), F32)
    for col in range(BLOCKS):
        flat[0, 128 * col : 128 * col + 128, :] = jnp.concatenate([direct[col], pad], axis=0).T
    flat[0, DA : DA + 8, :] = jnp.zeros((8, 128), F32)
    for third in (1, 2):
        flat[third] = pltpu.roll(flat[0], 40 * third, 1)
    send[:, :GRADS] = jnp.broadcast_to(own[None, :GRADS], (CHIPS, GRADS, 8, 128))
    for here in (0, 1):

        @pl.when(kind == here)
        def _():
            for n in range(CHIPS):
                first = 36 * n + 18 * ((here + n % 4 + n // 4) % 2)
                thirds = [flat[t, first + 6 * t : first + 6 * t + 8, :] for t in range(3)]
                send[n, GRADS] = thirds[0] + thirds[1] + thirds[2]


def spread(done, twin):
    vmem = pl.BlockSpec(memory_space=pltpu.VMEM)
    return pl.pallas_call(
        spread_kernel,
        out_shape=(
            jax.ShapeDtypeStruct((CHIPS, GRADS + 1, 8, 128), F32),
            jax.ShapeDtypeStruct((BLOCKS, 40, 128), F32),
            jax.ShapeDtypeStruct((8, 128), F32),
        ),
        in_specs=[vmem, vmem],
        out_specs=(vmem,) * 3,
        scratch_shapes=[pltpu.VMEM((3, DA + 8, 128), F32)],
        compiler_params=pltpu.CompilerParams(vmem_limit_bytes=16 * 2**20),
        name="spread",
    )(done, twin)


def rows_kernel(got, direct, total_ref, out, turned):
    group, xl, core, _ = position()
    total = total_ref[0:1, 0:1]
    for n in range(CHIPS):
        for third in range(3):
            rows = slice(6 * third, 6 * third + 6)
            for to, first, size in ((4, 0, 32), (0, 32, 4)) if n % 2 else ((0, 0, 36),):
                first = first + 40 * third
                turned[rows, 36 * n + to : 36 * n + to + size] = got[n, GRADS, 0:6, first : first + size]
    start = 72 * group + 36 * xl + 18 * core
    block = (lax.broadcasted_iota(jnp.int32, (18, 128), 0) + start) // 128
    for here in range(4):

        @pl.when(2 * xl + core == here)
        def _():
            first = (0, 18, 0, 14)[here]
            for col in range(BLOCKS):
                step = col - block
                step = jnp.where(step < 0, step + BLOCKS, step)
                lanes = slice(128 * col, 128 * col + 128)
                if here == 2:
                    straight = jnp.concatenate([direct[col, 32:36, :], direct[col, 0:14, :]], axis=0)
                else:
                    straight = direct[col, first : first + 18, :]
                value = jnp.where(step < HALF, straight, turned[:18, lanes]) / total
                for i in range(18):
                    out[i, :, lanes] = value[i : i + 1, :]


def factor_rows(got, direct, total):
    vmem = pl.BlockSpec(memory_space=pltpu.VMEM)
    out = pl.pallas_call(
        rows_kernel,
        out_shape=jax.ShapeDtypeStruct((18, 1, DA), F32),
        in_specs=[vmem] * 3,
        scratch_shapes=[pltpu.VMEM((24, DA), F32)],
        compiler_params=pltpu.CompilerParams(vmem_limit_bytes=16 * 2**20),
        cost_estimate=pl.CostEstimate(flops=10**6, bytes_accessed=2**20, transcendentals=0),
        name="factor_rows",
    )(got, direct, total)
    return out.reshape(1, 18, DA)


def precond_kernel(got, other, total_ref, basis_a, basis_g, eig_a, eig_g, g_factor, precond):
    kind = position()[3]
    total = total_ref[0:1, 0:1]
    shape = (16, 2, GRADS + 1, 8, 128)
    both = (got[...].reshape(shape), other[...].reshape(shape))
    columns = []
    for col in range(WIDTH // 128):
        n, rest = divmod(col, 5)
        low, rest = (rest < 3), (rest if rest < 3 else rest - 3)
        tiles = jnp.where((kind == 0) == low, both[0][:, n, rest], both[1][:, n, rest])
        columns.append(tiles.reshape(128, 128) / total)
    g_factor[0] = columns[-1]
    grad = jnp.concatenate([c.astype(BF16) for c in columns[:-1]], axis=1)
    left = lax.dot_general(basis_g[0], grad, (((0,), (0,)), ((), ())), preferred_element_type=F32).astype(BF16)
    rotated = jnp.dot(left, basis_a[0], preferred_element_type=F32)
    eig_rows = jnp.broadcast_to(eig_g[...], (DG, DG)).T[:, 0:1]
    scaled = (rotated / (eig_rows * eig_a[...] + 0.001)).astype(BF16)
    inner = jnp.dot(basis_g[0], scaled, preferred_element_type=F32).astype(BF16)
    precond[0] = lax.dot_general(inner, basis_a[0], (((1,), (1,)), ((), ())), preferred_element_type=F32)


def precondition(got, other, total, basis_a, basis_g, eig_a, eig_g):
    vmem = pl.BlockSpec(memory_space=pltpu.VMEM)
    return pl.pallas_call(
        precond_kernel,
        out_shape=(jax.ShapeDtypeStruct((1, DG, DG), F32), jax.ShapeDtypeStruct((1, DG, DA), F32)),
        in_specs=[vmem] * 7,
        compiler_params=pltpu.CompilerParams(vmem_limit_bytes=16 * 2**20),
        name="precondition",
    )(got, other, total, basis_a, basis_g, eig_a, eig_g)


def swap_cores(value):
    return lax.ppermute(value, "dp", [(i, i ^ 1) for i in range(64)])


def group_sums(value):
    value = value + lax.ppermute(value, "grp", [(i, i ^ 1) for i in range(4)])
    far = lax.ppermute(value, "grp", [(i, i ^ 3) for i in range(4)])
    twin = swap_cores(value)
    twin_far = lax.ppermute(value, ("dp", "grp"), [(i, i ^ 7) for i in range(256)])
    return value + far, twin + twin_far


def exchange(value, groups):
    return lax.all_to_all(value, "dp", 0, 0, axis_index_groups=groups, tiled=True)


def on_device(patches, out_grads, counts, basis_a, basis_g, eig_a, eig_g):
    mine, theirs = gram(patches, out_grads, counts)
    line = collect(exchange(mine + swap_cores(theirs), FIRST))
    part = collect(exchange(line, SECOND))
    send, direct, total = spread(*group_sums(part))
    got = exchange(send, CHIP_GROUPS)
    other = swap_cores(got)
    a_factor = factor_rows(got, direct, total)
    g_factor, precond = precondition(got, other, total, basis_a, basis_g, eig_a, eig_g)
    return a_factor, g_factor, precond


def solution(mesh):
    both = ("dp", "grp")
    placed = (P(None, both, None), P(None, both, None), P(both), P(), P(), P(), P())
    return jax.shard_map(
        on_device,
        mesh=mesh,
        in_specs=placed,
        out_specs=(P(None, "dp", None), P(), P()),
        check_vma=False,
    )
```

```python
import jax
import jax.numpy as jnp
from jax import lax
from jax.experimental import pallas as pl
from jax.experimental.pallas import tpu as pltpu
from jax.sharding import PartitionSpec as P

DA, DG, ROWS = 1152, 128, 2048
WIDTH = DA + DG
PARTS = (0, 512, ROWS)
BLOCKS = DA // 128
HALF = BLOCKS // 2 + 1
CHIPS, SLOTS, GRADS = 32, 14, 3
LOW = SLOTS - GRADS
CHIP_GROUPS = [[2 * n + core for n in range(CHIPS)] for core in (0, 1)]
FIRST = [[32 * zl + 8 * y + 2 * x for x in range(4)] for zl in range(2) for y in range(4)]
FIRST += [[32 * zl + 8 * y + 2 * x + 1 for y in range(4)] for zl in range(2) for x in range(4)]
SECOND = [[32 * zl + 8 * y + 2 * x for zl in range(2) for y in range(4)] for x in range(4)]
SECOND += [[32 * zl + 8 * y + 2 * x + 1 for zl in range(2) for x in range(4)] for y in range(4)]
HBM = pltpu.MemorySpace.HBM
F32, BF16 = jnp.float32, jnp.bfloat16


def factor_slot(v):
    return (0, GRADS + v) if v < LOW else (1, GRADS - 1 + v - LOW)


def factor_places(row8, step):
    group, within = divmod(row8, 9)
    if within == 4:
        core, slot = factor_slot(4 * HALF + step // 2)
        to = slice(4 * (step % 2), 4 * (step % 2) + 4)
        for xl in (0, 1):
            yield (core, 2 * group + xl, slot, to), slice(4 * xl, 4 * xl + 4)
    else:
        xl = within // 5
        core, slot = factor_slot((within - 5 * xl) * HALF + step)
        yield (core, 2 * group + xl, slot, slice(0, 8)), slice(0, 8)


def grad_place(row8, col):
    chip, rest = divmod(row8 * 10 + col, 5)
    return (0, chip, rest, slice(0, 8)) if rest < 3 else (1, chip, rest - 3, slice(0, 8))


def position():
    dp = lax.axis_index("dp")
    return lax.div(dp, 4), lax.rem(lax.div(dp, 2), 2), lax.rem(dp, 2)


def ordered(core, chip):
    zl, y, x = chip // 16, chip // 4 % 4, chip % 4
    return (y, 4 * zl + x) if core else (x, 4 * zl + y)


def products(part, z, zt, acc):
    depth = slice(PARTS[part], PARTS[part + 1])

    def put(place, tile):
        place = place[:1] + ordered(*place[:2]) + place[2:]
        acc[place] = acc[place] + tile if part else tile

    for col0 in range(0, BLOCKS + 1, 2):
        wanted = sorted({(c - s) % BLOCKS for c in (col0, col0 + 1) if c < BLOCKS for s in range(HALF)}) + [BLOCKS]
        runs = []
        for i in wanted:
            if runs and runs[-1][-1] == i - 1:
                runs[-1].append(i)
            else:
                runs.append([i])
        for run in runs:
            w = jnp.dot(
                zt[128 * run[0] : 128 * run[-1] + 128, depth],
                z[depth, 128 * col0 : 128 * col0 + 256],
                preferred_element_type=F32,
            )
            for u in range(16 * len(run)):
                row8 = 16 * run[0] + u
                for v in (0, 1):
                    tile = w[8 * u : 8 * u + 8, 128 * v : 128 * v + 128]
                    if row8 >= DA // 8:
                        put(grad_place(row8 - DA // 8, col0 + v), tile)
                    elif col0 + v < BLOCKS and (col0 + v - row8 // 16) % BLOCKS < HALF:
                        for place, rows in factor_places(row8, (col0 + v - row8 // 16) % BLOCKS):
                            put(place, tile[rows])


def gram_kernel(count_ref, x_hbm, y_hbm, mine, theirs, z, zt, acc, in_sem, out_sem):
    copies = []
    for k in range(len(PARTS) - 1):
        rows = pl.ds(PARTS[k], PARTS[k + 1] - PARTS[k])
        copies.append(
            (
                pltpu.make_async_copy(x_hbm.at[0, rows, :], z.at[rows, pl.ds(0, DA)], in_sem.at[k, 0]),
                pltpu.make_async_copy(y_hbm.at[0, rows, :], z.at[rows, pl.ds(DA, DG)], in_sem.at[k, 1]),
            )
        )
        for copy in copies[k]:
            copy.start()
    count, core = count_ref[0], lax.rem(lax.axis_index("dp"), 2)
    acc[1, :, :, SLOTS - 1, 4:8, :] = jnp.full((4, 8, 4, 128), count.astype(F32))
    for k in range(len(PARTS) - 1):
        for copy in copies[k]:
            copy.wait()
        here = slice(PARTS[k], PARTS[k + 1])
        row = lax.broadcasted_iota(jnp.int32, (PARTS[k + 1] - PARTS[k], 1), 0) + PARTS[k]
        zt[:, here] = jnp.where(row < count, z[here, :], jnp.zeros((), BF16)).T
        products(k, z, zt, acc)
    first = pltpu.make_async_copy(acc.at[1 - core], theirs, out_sem.at[0])
    second = pltpu.make_async_copy(acc.at[core], mine, out_sem.at[1])
    first.start()
    second.start()
    first.wait()
    second.wait()


def gram(patches, out_grads, counts):
    half = jax.ShapeDtypeStruct((4, 8, SLOTS, 8, 128), F32)
    return pl.pallas_call(
        gram_kernel,
        out_shape=(half, half),
        in_specs=[pl.BlockSpec(memory_space=pltpu.SMEM)] + [pl.BlockSpec(memory_space=HBM)] * 2,
        out_specs=(pl.BlockSpec(memory_space=HBM),) * 2,
        scratch_shapes=[
            pltpu.VMEM((ROWS, WIDTH), BF16),
            pltpu.VMEM((WIDTH, ROWS), BF16),
            pltpu.VMEM((2, 4, 8, SLOTS, 8, 128), F32),
            pltpu.SemaphoreType.DMA((len(PARTS) - 1, 2)),
            pltpu.SemaphoreType.DMA((2,)),
        ],
        compiler_params=pltpu.CompilerParams(vmem_limit_bytes=48 * 2**20),
        cost_estimate=pl.CostEstimate(flops=2 * ROWS * WIDTH * WIDTH, bytes_accessed=10 * 2**20, transcendentals=0),
        name="gram",
    )(counts, patches, out_grads)


def collect_kernel(met, out):
    total = met[0]
    for n in range(1, met.shape[0]):
        total = total + met[n]
    out[...] = total


def collect(met):
    return pl.pallas_call(
        collect_kernel,
        out_shape=jax.ShapeDtypeStruct(met.shape[1:], F32),
        compiler_params=pltpu.CompilerParams(vmem_limit_bytes=16 * 2**20),
        name="collect",
    )(met)


def spread_kernel(done, twin, send, direct, total, flat):
    group, xl, core = position()
    own, other = done[...], twin[...]
    low = jnp.where(core == 0, own, other)
    high = jnp.where(core == 0, other, own)
    total[...] = jnp.broadcast_to(high[SLOTS - 1, 4:5], (8, 128))
    direct[...] = jnp.zeros_like(direct)
    shared = (9 * group + 4) // 16
    for v in range(4 * HALF + HALF // 2 + 1):
        here, slot = factor_slot(v)
        tile = high[slot] if here else low[slot]
        u, step = divmod(v, HALF)
        if u < 4:
            col = lax.rem((9 * group + 5 * xl + u) // 16 + step, BLOCKS)
            direct[col, 8 * u : 8 * u + 8, :] = tile
        else:
            direct[lax.rem(shared + 2 * step, BLOCKS), 32:36, :] = tile[0:4]
            if 2 * step + 1 < HALF:
                direct[lax.rem(shared + 2 * step + 1, BLOCKS), 32:36, :] = tile[4:8]
    pad = jnp.zeros((128 - 40, 128), F32)
    for col in range(BLOCKS):
        flat[0, 128 * col : 128 * col + 128, :] = jnp.concatenate([direct[col], pad], axis=0).T
    flat[0, DA : DA + 8, :] = jnp.zeros((8, 128), F32)
    for third in (1, 2):
        flat[third] = pltpu.roll(flat[0], 40 * third, 1)
    send[:, :GRADS] = jnp.broadcast_to(own[None, :GRADS], (CHIPS, GRADS, 8, 128))
    for here in (0, 1):

        @pl.when(core == here)
        def _():
            for n in range(CHIPS):
                first = 36 * n + 18 * here
                thirds = [flat[t, first + 6 * t : first + 6 * t + 8, :] for t in range(3)]
                send[n, GRADS] = thirds[0] + thirds[1] + thirds[2]


def spread(done, twin):
    vmem = pl.BlockSpec(memory_space=pltpu.VMEM)
    return pl.pallas_call(
        spread_kernel,
        out_shape=(
            jax.ShapeDtypeStruct((CHIPS, GRADS + 1, 8, 128), F32),
            jax.ShapeDtypeStruct((BLOCKS, 40, 128), F32),
            jax.ShapeDtypeStruct((8, 128), F32),
        ),
        in_specs=[vmem, vmem],
        out_specs=(vmem,) * 3,
        scratch_shapes=[pltpu.VMEM((3, DA + 8, 128), F32)],
        compiler_params=pltpu.CompilerParams(vmem_limit_bytes=16 * 2**20),
        name="spread",
    )(done, twin)


def rows_kernel(got, direct, total_ref, out, turned):
    group, xl, core = position()
    total = total_ref[0:1, 0:1]
    for n in range(CHIPS):
        for third in range(3):
            rows = slice(6 * third, 6 * third + 6)
            for to, first, size in ((4, 0, 32), (0, 32, 4)) if n % 2 else ((0, 0, 36),):
                first = first + 40 * third
                turned[rows, 36 * n + to : 36 * n + to + size] = got[n, GRADS, 0:6, first : first + size]
    start = 72 * group + 36 * xl + 18 * core
    block = (lax.broadcasted_iota(jnp.int32, (18, 128), 0) + start) // 128
    for here in range(4):

        @pl.when(2 * xl + core == here)
        def _():
            first = (0, 18, 0, 14)[here]
            for col in range(BLOCKS):
                step = col - block
                step = jnp.where(step < 0, step + BLOCKS, step)
                lanes = slice(128 * col, 128 * col + 128)
                if here == 2:
                    straight = jnp.concatenate([direct[col, 32:36, :], direct[col, 0:14, :]], axis=0)
                else:
                    straight = direct[col, first : first + 18, :]
                value = jnp.where(step < HALF, straight, turned[:18, lanes]) / total
                for i in range(18):
                    out[i, :, lanes] = value[i : i + 1, :]


def factor_rows(got, direct, total):
    vmem = pl.BlockSpec(memory_space=pltpu.VMEM)
    out = pl.pallas_call(
        rows_kernel,
        out_shape=jax.ShapeDtypeStruct((18, 1, DA), F32),
        in_specs=[vmem] * 3,
        scratch_shapes=[pltpu.VMEM((24, DA), F32)],
        compiler_params=pltpu.CompilerParams(vmem_limit_bytes=16 * 2**20),
        cost_estimate=pl.CostEstimate(flops=10**6, bytes_accessed=2**20, transcendentals=0),
        name="factor_rows",
    )(got, direct, total)
    return out.reshape(1, 18, DA)


def precond_kernel(got, other, total_ref, basis_a, basis_g, eig_a, eig_g, g_factor, precond):
    core = lax.rem(lax.axis_index("dp"), 2)
    total = total_ref[0:1, 0:1]
    shape = (16, 2, GRADS + 1, 8, 128)
    both = (got[...].reshape(shape), other[...].reshape(shape))
    columns = []
    for col in range(WIDTH // 128):
        n, rest = divmod(col, 5)
        low, rest = (rest < 3), (rest if rest < 3 else rest - 3)
        tiles = jnp.where((core == 0) == low, both[0][:, n, rest], both[1][:, n, rest])
        columns.append(tiles.reshape(128, 128) / total)
    g_factor[0] = columns[-1]
    grad = jnp.concatenate([c.astype(BF16) for c in columns[:-1]], axis=1)
    left = lax.dot_general(basis_g[0], grad, (((0,), (0,)), ((), ())), preferred_element_type=F32).astype(BF16)
    rotated = jnp.dot(left, basis_a[0], preferred_element_type=F32)
    eig_rows = jnp.broadcast_to(eig_g[...], (DG, DG)).T[:, 0:1]
    scaled = (rotated / (eig_rows * eig_a[...] + 0.001)).astype(BF16)
    inner = jnp.dot(basis_g[0], scaled, preferred_element_type=F32).astype(BF16)
    precond[0] = lax.dot_general(inner, basis_a[0], (((1,), (1,)), ((), ())), preferred_element_type=F32)


def precondition(got, other, total, basis_a, basis_g, eig_a, eig_g):
    vmem = pl.BlockSpec(memory_space=pltpu.VMEM)
    return pl.pallas_call(
        precond_kernel,
        out_shape=(jax.ShapeDtypeStruct((1, DG, DG), F32), jax.ShapeDtypeStruct((1, DG, DA), F32)),
        in_specs=[vmem] * 7,
        compiler_params=pltpu.CompilerParams(vmem_limit_bytes=16 * 2**20),
        name="precondition",
    )(got, other, total, basis_a, basis_g, eig_a, eig_g)


def swap_cores(value):
    return lax.ppermute(value, "dp", [(i, i ^ 1) for i in range(64)])


def group_sum(value):
    for k in (1, 3):
        value = value + lax.ppermute(value, "grp", [(i, i ^ k) for i in range(4)])
    return value


def exchange(value, groups):
    return lax.all_to_all(value, "dp", 0, 0, axis_index_groups=groups, tiled=True)


def on_device(patches, out_grads, counts, basis_a, basis_g, eig_a, eig_g):
    mine, theirs = gram(patches, out_grads, counts)
    line = collect(exchange(mine + swap_cores(theirs), FIRST))
    done = group_sum(collect(exchange(line, SECOND)))
    send, direct, total = spread(done, swap_cores(done))
    got = exchange(send, CHIP_GROUPS)
    other = swap_cores(got)
    a_factor = factor_rows(got, direct, total)
    g_factor, precond = precondition(got, other, total, basis_a, basis_g, eig_a, eig_g)
    return a_factor, g_factor, precond


def solution(mesh):
    both = ("dp", "grp")
    placed = (P(None, both, None), P(None, both, None), P(both), P(), P(), P(), P())
    return jax.shard_map(
        on_device,
        mesh=mesh,
        in_specs=placed,
        out_specs=(P(None, "dp", None), P(), P()),
        check_vma=False,
    )
```

```python
import jax
import jax.numpy as jnp
from jax import lax
from jax.experimental import pallas as pl
from jax.experimental.pallas import tpu as pltpu
from jax.sharding import PartitionSpec as P

DA, DG, ROWS = 1152, 128, 2048
WIDTH = DA + DG
PARTS = (0, 512, ROWS)
BLOCKS = DA // 128
HALF = BLOCKS // 2 + 1
CHIPS, SLOTS, GRADS = 32, 14, 3
LOW = SLOTS - GRADS
CHIP_GROUPS = [[2 * n + core for n in range(CHIPS)] for core in (0, 1)]
FIRST = [[32 * zl + 8 * y + 2 * x for x in range(4)] for zl in range(2) for y in range(4)]
FIRST += [[32 * zl + 8 * y + 2 * x + 1 for y in range(4)] for zl in range(2) for x in range(4)]
SECOND = [[32 * zl + 8 * y + 2 * x for zl in range(2) for y in range(4)] for x in range(4)]
SECOND += [[32 * zl + 8 * y + 2 * x + 1 for zl in range(2) for x in range(4)] for y in range(4)]
HBM = pltpu.MemorySpace.HBM
F32, BF16 = jnp.float32, jnp.bfloat16


def factor_slot(v):
    return (0, GRADS + v) if v < LOW else (1, GRADS - 1 + v - LOW)


def factor_places(row8, step):
    group, within = divmod(row8, 9)
    if within == 4:
        core, slot = factor_slot(4 * HALF + step // 2)
        to = slice(4 * (step % 2), 4 * (step % 2) + 4)
        for xl in (0, 1):
            yield (core, 2 * group + xl, slot, to), slice(4 * xl, 4 * xl + 4)
    else:
        xl = within // 5
        core, slot = factor_slot((within - 5 * xl) * HALF + step)
        yield (core, 2 * group + xl, slot, slice(0, 8)), slice(0, 8)


def grad_place(row8, col):
    chip, rest = divmod(row8 * 10 + col, 5)
    return (0, chip, rest, slice(0, 8)) if rest < 3 else (1, chip, rest - 3, slice(0, 8))


def position():
    dp = lax.axis_index("dp")
    return lax.div(dp, 4), lax.rem(lax.div(dp, 2), 2), lax.rem(dp, 2)


def ordered(core, chip):
    zl, y, x = chip // 16, chip // 4 % 4, chip % 4
    return (y, 4 * zl + x) if core else (x, 4 * zl + y)


def products(part, z, zt, acc):
    depth = slice(PARTS[part], PARTS[part + 1])

    def put(place, tile):
        place = place[:1] + ordered(*place[:2]) + place[2:]
        acc[place] = acc[place] + tile if part else tile

    for col0 in range(0, BLOCKS + 1, 2):
        wanted = sorted({(c - s) % BLOCKS for c in (col0, col0 + 1) if c < BLOCKS for s in range(HALF)}) + [BLOCKS]
        runs = []
        for i in wanted:
            if runs and runs[-1][-1] == i - 1:
                runs[-1].append(i)
            else:
                runs.append([i])
        for run in runs:
            w = jnp.dot(
                zt[128 * run[0] : 128 * run[-1] + 128, depth],
                z[depth, 128 * col0 : 128 * col0 + 256],
                preferred_element_type=F32,
            )
            for u in range(16 * len(run)):
                row8 = 16 * run[0] + u
                for v in (0, 1):
                    tile = w[8 * u : 8 * u + 8, 128 * v : 128 * v + 128]
                    if row8 >= DA // 8:
                        put(grad_place(row8 - DA // 8, col0 + v), tile)
                    elif col0 + v < BLOCKS and (col0 + v - row8 // 16) % BLOCKS < HALF:
                        for place, rows in factor_places(row8, (col0 + v - row8 // 16) % BLOCKS):
                            put(place, tile[rows])


def gram_kernel(count_ref, x_hbm, y_hbm, mine, theirs, z, zt, acc, in_sem, out_sem):
    copies = []
    for k in range(len(PARTS) - 1):
        rows = pl.ds(PARTS[k], PARTS[k + 1] - PARTS[k])
        copies.append(
            (
                pltpu.make_async_copy(x_hbm.at[0, rows, :], z.at[rows, pl.ds(0, DA)], in_sem.at[k, 0]),
                pltpu.make_async_copy(y_hbm.at[0, rows, :], z.at[rows, pl.ds(DA, DG)], in_sem.at[k, 1]),
            )
        )
        for copy in copies[k]:
            copy.start()
    count, core = count_ref[0], lax.rem(lax.axis_index("dp"), 2)
    acc[1, :, :, SLOTS - 1, 4:8, :] = jnp.full((4, 8, 4, 128), count.astype(F32))
    for k in range(len(PARTS) - 1):
        for copy in copies[k]:
            copy.wait()
        here = slice(PARTS[k], PARTS[k + 1])
        row = lax.broadcasted_iota(jnp.int32, (PARTS[k + 1] - PARTS[k], 1), 0) + PARTS[k]
        zt[:, here] = jnp.where(row < count, z[here, :], jnp.zeros((), BF16)).T
        products(k, z, zt, acc)
    first = pltpu.make_async_copy(acc.at[1 - core], theirs, out_sem.at[0])
    second = pltpu.make_async_copy(acc.at[core], mine, out_sem.at[1])
    first.start()
    second.start()
    first.wait()
    second.wait()


def gram(patches, out_grads, counts):
    half = jax.ShapeDtypeStruct((4, 8, SLOTS, 8, 128), F32)
    return pl.pallas_call(
        gram_kernel,
        out_shape=(half, half),
        in_specs=[pl.BlockSpec(memory_space=pltpu.SMEM)] + [pl.BlockSpec(memory_space=HBM)] * 2,
        out_specs=(pl.BlockSpec(memory_space=HBM),) * 2,
        scratch_shapes=[
            pltpu.VMEM((ROWS, WIDTH), BF16),
            pltpu.VMEM((WIDTH, ROWS), BF16),
            pltpu.VMEM((2, 4, 8, SLOTS, 8, 128), F32),
            pltpu.SemaphoreType.DMA((len(PARTS) - 1, 2)),
            pltpu.SemaphoreType.DMA((2,)),
        ],
        compiler_params=pltpu.CompilerParams(vmem_limit_bytes=48 * 2**20),
        cost_estimate=pl.CostEstimate(flops=2 * ROWS * WIDTH * WIDTH, bytes_accessed=10 * 2**20, transcendentals=0),
        name="gram",
    )(counts, *(pltpu.with_memory_space_constraint(v, HBM) for v in (patches, out_grads)))


def collect_kernel(met, out):
    total = met[0]
    for n in range(1, met.shape[0]):
        total = total + met[n]
    out[...] = total


def collect(met):
    return pl.pallas_call(
        collect_kernel,
        out_shape=jax.ShapeDtypeStruct(met.shape[1:], F32),
        compiler_params=pltpu.CompilerParams(vmem_limit_bytes=16 * 2**20),
        name="collect",
    )(met)


def spread_kernel(done, twin, send, direct, total, flat):
    group, xl, core = position()
    own, other = done[...], twin[...]
    low = jnp.where(core == 0, own, other)
    high = jnp.where(core == 0, other, own)
    total[...] = jnp.broadcast_to(high[SLOTS - 1, 4:5], (8, 128))
    direct[...] = jnp.zeros_like(direct)
    shared = (9 * group + 4) // 16
    for v in range(4 * HALF + HALF // 2 + 1):
        here, slot = factor_slot(v)
        tile = high[slot] if here else low[slot]
        u, step = divmod(v, HALF)
        if u < 4:
            col = lax.rem((9 * group + 5 * xl + u) // 16 + step, BLOCKS)
            direct[col, 8 * u : 8 * u + 8, :] = tile
        else:
            direct[lax.rem(shared + 2 * step, BLOCKS), 32:36, :] = tile[0:4]
            if 2 * step + 1 < HALF:
                direct[lax.rem(shared + 2 * step + 1, BLOCKS), 32:36, :] = tile[4:8]
    pad = jnp.zeros((128 - 40, 128), F32)
    for col in range(BLOCKS):
        flat[0, 128 * col : 128 * col + 128, :] = jnp.concatenate([direct[col], pad], axis=0).T
    flat[0, DA : DA + 8, :] = jnp.zeros((8, 128), F32)
    for third in (1, 2):
        flat[third] = pltpu.roll(flat[0], 40 * third, 1)
    send[:, :GRADS] = jnp.broadcast_to(own[None, :GRADS], (CHIPS, GRADS, 8, 128))
    for here in (0, 1):

        @pl.when(core == here)
        def _():
            for n in range(CHIPS):
                first = 36 * n + 18 * here
                thirds = [flat[t, first + 6 * t : first + 6 * t + 8, :] for t in range(3)]
                send[n, GRADS] = thirds[0] + thirds[1] + thirds[2]


def spread(done, twin):
    vmem = pl.BlockSpec(memory_space=pltpu.VMEM)
    return pl.pallas_call(
        spread_kernel,
        out_shape=(
            jax.ShapeDtypeStruct((CHIPS, GRADS + 1, 8, 128), F32),
            jax.ShapeDtypeStruct((BLOCKS, 40, 128), F32),
            jax.ShapeDtypeStruct((8, 128), F32),
        ),
        in_specs=[vmem, vmem],
        out_specs=(vmem,) * 3,
        scratch_shapes=[pltpu.VMEM((3, DA + 8, 128), F32)],
        compiler_params=pltpu.CompilerParams(vmem_limit_bytes=16 * 2**20),
        name="spread",
    )(done, twin)


def rows_kernel(got, direct, total_ref, out, turned):
    group, xl, core = position()
    total = total_ref[0:1, 0:1]
    for n in range(CHIPS):
        for third in range(3):
            rows = slice(6 * third, 6 * third + 6)
            for to, first, size in ((4, 0, 32), (0, 32, 4)) if n % 2 else ((0, 0, 36),):
                first = first + 40 * third
                turned[rows, 36 * n + to : 36 * n + to + size] = got[n, GRADS, 0:6, first : first + size]
    start = 72 * group + 36 * xl + 18 * core
    block = (lax.broadcasted_iota(jnp.int32, (18, 128), 0) + start) // 128
    for here in range(4):

        @pl.when(2 * xl + core == here)
        def _():
            first = (0, 18, 0, 14)[here]
            for col in range(BLOCKS):
                step = col - block
                step = jnp.where(step < 0, step + BLOCKS, step)
                lanes = slice(128 * col, 128 * col + 128)
                if here == 2:
                    straight = jnp.concatenate([direct[col, 32:36, :], direct[col, 0:14, :]], axis=0)
                else:
                    straight = direct[col, first : first + 18, :]
                value = jnp.where(step < HALF, straight, turned[:18, lanes]) / total
                for i in range(18):
                    out[i, :, lanes] = value[i : i + 1, :]


def factor_rows(got, direct, total):
    vmem = pl.BlockSpec(memory_space=pltpu.VMEM)
    out = pl.pallas_call(
        rows_kernel,
        out_shape=jax.ShapeDtypeStruct((18, 1, DA), F32),
        in_specs=[vmem] * 3,
        scratch_shapes=[pltpu.VMEM((24, DA), F32)],
        compiler_params=pltpu.CompilerParams(vmem_limit_bytes=16 * 2**20),
        cost_estimate=pl.CostEstimate(flops=10**6, bytes_accessed=2**20, transcendentals=0),
        name="factor_rows",
    )(got, direct, total)
    return out.reshape(1, 18, DA)


def precond_kernel(got, other, total_ref, basis_a, basis_g, eig_a, eig_g, g_factor, precond):
    core = lax.rem(lax.axis_index("dp"), 2)
    total = total_ref[0:1, 0:1]
    shape = (16, 2, GRADS + 1, 8, 128)
    both = (got[...].reshape(shape), other[...].reshape(shape))
    columns = []
    for col in range(WIDTH // 128):
        n, rest = divmod(col, 5)
        low, rest = (rest < 3), (rest if rest < 3 else rest - 3)
        tiles = jnp.where((core == 0) == low, both[0][:, n, rest], both[1][:, n, rest])
        columns.append(tiles.reshape(128, 128) / total)
    g_factor[0] = columns[-1]
    grad = jnp.concatenate([c.astype(BF16) for c in columns[:-1]], axis=1)
    left = lax.dot_general(basis_g[0], grad, (((0,), (0,)), ((), ())), preferred_element_type=F32).astype(BF16)
    rotated = jnp.dot(left, basis_a[0], preferred_element_type=F32)
    eig_rows = jnp.broadcast_to(eig_g[...], (DG, DG)).T[:, 0:1]
    scaled = (rotated / (eig_rows * eig_a[...] + 0.001)).astype(BF16)
    inner = jnp.dot(basis_g[0], scaled, preferred_element_type=F32).astype(BF16)
    precond[0] = lax.dot_general(inner, basis_a[0], (((1,), (1,)), ((), ())), preferred_element_type=F32)


def precondition(got, other, total, basis_a, basis_g, eig_a, eig_g):
    vmem = pl.BlockSpec(memory_space=pltpu.VMEM)
    return pl.pallas_call(
        precond_kernel,
        out_shape=(jax.ShapeDtypeStruct((1, DG, DG), F32), jax.ShapeDtypeStruct((1, DG, DA), F32)),
        in_specs=[vmem] * 7,
        compiler_params=pltpu.CompilerParams(vmem_limit_bytes=16 * 2**20),
        name="precondition",
    )(got, other, total, basis_a, basis_g, eig_a, eig_g)


def swap_cores(value):
    return lax.ppermute(value, "dp", [(i, i ^ 1) for i in range(64)])


def group_sum(value):
    for k in (1, 3):
        value = value + lax.ppermute(value, "grp", [(i, i ^ k) for i in range(4)])
    return value


def exchange(value, groups):
    return lax.all_to_all(value, "dp", 0, 0, axis_index_groups=groups, tiled=True)


def on_device(patches, out_grads, counts, basis_a, basis_g, eig_a, eig_g):
    mine, theirs = gram(patches, out_grads, counts)
    line = collect(exchange(mine + swap_cores(theirs), FIRST))
    done = group_sum(collect(exchange(line, SECOND)))
    send, direct, total = spread(done, swap_cores(done))
    got = exchange(send, CHIP_GROUPS)
    other = swap_cores(got)
    a_factor = factor_rows(got, direct, total)
    g_factor, precond = precondition(got, other, total, basis_a, basis_g, eig_a, eig_g)
    return a_factor, g_factor, precond


def solution(mesh):
    both = ("dp", "grp")
    placed = (P(None, both, None), P(None, both, None), P(both), P(), P(), P(), P())
    return jax.shard_map(
        on_device,
        mesh=mesh,
        in_specs=placed,
        out_specs=(P(None, "dp", None), P(), P()),
        check_vma=False,
    )
```

```python
import jax
import jax.numpy as jnp
from jax import lax
from jax.experimental import pallas as pl
from jax.experimental.pallas import tpu as pltpu
from jax.sharding import PartitionSpec as P

DA, DG, ROWS = 1152, 128, 2048
WIDTH = DA + DG
PARTS = (0, 512, ROWS)
BLOCKS = DA // 128
HALF = BLOCKS // 2 + 1
CHIPS, SLOTS, GRADS = 32, 14, 3
LOW = SLOTS - GRADS
CHIP_GROUPS = [[2 * n + core for n in range(CHIPS)] for core in (0, 1)]
FIRST = [[32 * zl + 8 * y + 2 * x for x in range(4)] for zl in range(2) for y in range(4)]
FIRST += [[32 * zl + 8 * y + 2 * x + 1 for y in range(4)] for zl in range(2) for x in range(4)]
SECOND = [[32 * zl + 8 * y + 2 * x for zl in range(2) for y in range(4)] for x in range(4)]
SECOND += [[32 * zl + 8 * y + 2 * x + 1 for zl in range(2) for x in range(4)] for y in range(4)]
HBM = pltpu.MemorySpace.HBM
F32, BF16 = jnp.float32, jnp.bfloat16


def factor_slot(v):
    return (0, GRADS + v) if v < LOW else (1, GRADS - 1 + v - LOW)


def factor_places(row8, step):
    group, within = divmod(row8, 9)
    if within == 4:
        core, slot = factor_slot(4 * HALF + step // 2)
        to = slice(4 * (step % 2), 4 * (step % 2) + 4)
        for xl in (0, 1):
            yield (core, 2 * group + xl, slot, to), slice(4 * xl, 4 * xl + 4)
    else:
        xl = within // 5
        core, slot = factor_slot((within - 5 * xl) * HALF + step)
        yield (core, 2 * group + xl, slot, slice(0, 8)), slice(0, 8)


def grad_place(row8, col):
    chip, rest = divmod(row8 * 10 + col, 5)
    return (0, chip, rest, slice(0, 8)) if rest < 3 else (1, chip, rest - 3, slice(0, 8))


def position():
    dp = lax.axis_index("dp")
    return lax.div(dp, 4), lax.rem(lax.div(dp, 2), 2), lax.rem(dp, 2)


def ordered(core, chip):
    zl, y, x = chip // 16, chip // 4 % 4, chip % 4
    return (y, 4 * zl + x) if core else (x, 4 * zl + y)


def products(part, z, zt, acc):
    depth = slice(PARTS[part], PARTS[part + 1])

    def put(place, tile):
        place = place[:1] + ordered(*place[:2]) + place[2:]
        acc[place] = acc[place] + tile if part else tile

    for col0 in range(0, BLOCKS + 1, 2):
        wanted = sorted({(c - s) % BLOCKS for c in (col0, col0 + 1) if c < BLOCKS for s in range(HALF)}) + [BLOCKS]
        runs = []
        for i in wanted:
            if runs and runs[-1][-1] == i - 1:
                runs[-1].append(i)
            else:
                runs.append([i])
        for run in runs:
            w = jnp.dot(
                zt[128 * run[0] : 128 * run[-1] + 128, depth],
                z[depth, 128 * col0 : 128 * col0 + 256],
                preferred_element_type=F32,
            )
            for u in range(16 * len(run)):
                row8 = 16 * run[0] + u
                for v in (0, 1):
                    tile = w[8 * u : 8 * u + 8, 128 * v : 128 * v + 128]
                    if row8 >= DA // 8:
                        put(grad_place(row8 - DA // 8, col0 + v), tile)
                    elif col0 + v < BLOCKS and (col0 + v - row8 // 16) % BLOCKS < HALF:
                        for place, rows in factor_places(row8, (col0 + v - row8 // 16) % BLOCKS):
                            put(place, tile[rows])


def gram_kernel(count_ref, x_hbm, y_hbm, mine, theirs, z, zt, acc, in_sem, out_sem):
    copies = []
    for k in range(len(PARTS) - 1):
        rows = pl.ds(PARTS[k], PARTS[k + 1] - PARTS[k])
        copies.append(
            (
                pltpu.make_async_copy(x_hbm.at[0, rows, :], z.at[rows, pl.ds(0, DA)], in_sem.at[k, 0]),
                pltpu.make_async_copy(y_hbm.at[0, rows, :], z.at[rows, pl.ds(DA, DG)], in_sem.at[k, 1]),
            )
        )
        for copy in copies[k]:
            copy.start()
    count, core = count_ref[0], lax.rem(lax.axis_index("dp"), 2)
    acc[1, :, :, SLOTS - 1, 4:8, :] = jnp.full((4, 8, 4, 128), count.astype(F32))
    for k in range(len(PARTS) - 1):
        for copy in copies[k]:
            copy.wait()
        here = slice(PARTS[k], PARTS[k + 1])
        row = lax.broadcasted_iota(jnp.int32, (PARTS[k + 1] - PARTS[k], 1), 0) + PARTS[k]
        zt[:, here] = jnp.where(row < count, z[here, :], jnp.zeros((), BF16)).T
        products(k, z, zt, acc)
    first = pltpu.make_async_copy(acc.at[1 - core], theirs, out_sem.at[0])
    second = pltpu.make_async_copy(acc.at[core], mine, out_sem.at[1])
    first.start()
    second.start()
    first.wait()
    second.wait()


def gram(patches, out_grads, counts):
    half = jax.ShapeDtypeStruct((4, 8, SLOTS, 8, 128), F32)
    return pl.pallas_call(
        gram_kernel,
        out_shape=(half, half),
        in_specs=[pl.BlockSpec(memory_space=pltpu.SMEM)] + [pl.BlockSpec(memory_space=HBM)] * 2,
        out_specs=(pl.BlockSpec(memory_space=HBM),) * 2,
        scratch_shapes=[
            pltpu.VMEM((ROWS, WIDTH), BF16),
            pltpu.VMEM((WIDTH, ROWS), BF16),
            pltpu.VMEM((2, 4, 8, SLOTS, 8, 128), F32),
            pltpu.SemaphoreType.DMA((len(PARTS) - 1, 2)),
            pltpu.SemaphoreType.DMA((2,)),
        ],
        compiler_params=pltpu.CompilerParams(vmem_limit_bytes=48 * 2**20),
        cost_estimate=pl.CostEstimate(flops=2 * ROWS * WIDTH * WIDTH, bytes_accessed=10 * 2**20, transcendentals=0),
        name="gram",
    )(counts, *(pltpu.with_memory_space_constraint(v, HBM) for v in (patches, out_grads)))


def collect_kernel(met, out):
    total = met[0]
    for n in range(1, met.shape[0]):
        total = total + met[n]
    out[...] = total


def collect(met):
    return pl.pallas_call(
        collect_kernel,
        out_shape=jax.ShapeDtypeStruct(met.shape[1:], F32),
        compiler_params=pltpu.CompilerParams(vmem_limit_bytes=16 * 2**20),
        name="collect",
    )(met)


def spread_kernel(done, twin, send, direct, total, flat):
    group, xl, core = position()
    own, other = done[...], twin[...]
    low = jnp.where(core == 0, own, other)
    high = jnp.where(core == 0, other, own)
    total[...] = jnp.broadcast_to(high[SLOTS - 1, 4:5], (8, 128))
    direct[...] = jnp.zeros_like(direct)
    shared = (9 * group + 4) // 16
    for v in range(4 * HALF + HALF // 2 + 1):
        here, slot = factor_slot(v)
        tile = high[slot] if here else low[slot]
        u, step = divmod(v, HALF)
        if u < 4:
            col = lax.rem((9 * group + 5 * xl + u) // 16 + step, BLOCKS)
            direct[col, 8 * u : 8 * u + 8, :] = tile
        else:
            direct[lax.rem(shared + 2 * step, BLOCKS), 32:36, :] = tile[0:4]
            if 2 * step + 1 < HALF:
                direct[lax.rem(shared + 2 * step + 1, BLOCKS), 32:36, :] = tile[4:8]
    pad = jnp.zeros((128 - 40, 128), F32)
    for col in range(BLOCKS):
        flat[0, 128 * col : 128 * col + 128, :] = jnp.concatenate([direct[col], pad], axis=0).T
    flat[0, DA : DA + 8, :] = jnp.zeros((8, 128), F32)
    for third in (1, 2):
        flat[third] = pltpu.roll(flat[0], 40 * third, 1)
    send[:, :GRADS] = jnp.broadcast_to(own[None, :GRADS], (CHIPS, GRADS, 8, 128))
    for here in (0, 1):

        @pl.when(core == here)
        def _():
            for n in range(CHIPS):
                first = 36 * n + 18 * here
                thirds = [flat[t, first + 6 * t : first + 6 * t + 8, :] for t in range(3)]
                send[n, GRADS] = thirds[0] + thirds[1] + thirds[2]


def spread(done, twin):
    vmem = pl.BlockSpec(memory_space=pltpu.VMEM)
    return pl.pallas_call(
        spread_kernel,
        out_shape=(
            jax.ShapeDtypeStruct((CHIPS, GRADS + 1, 8, 128), F32),
            jax.ShapeDtypeStruct((BLOCKS, 40, 128), F32),
            jax.ShapeDtypeStruct((8, 128), F32),
        ),
        in_specs=[vmem, vmem],
        out_specs=(vmem,) * 3,
        scratch_shapes=[pltpu.VMEM((3, DA + 8, 128), F32)],
        compiler_params=pltpu.CompilerParams(vmem_limit_bytes=16 * 2**20),
        name="spread",
    )(done, twin)


def rows_kernel(got, direct, total_ref, eig_a, eig_g, out, scale, turned):
    scale[...] = 1.0 / (jnp.broadcast_to(eig_g[...], (DG, DG)).T[:, 0:1] * eig_a[...] + 0.001)
    group, xl, core = position()
    total = total_ref[0:1, 0:1]
    for n in range(CHIPS):
        for third in range(3):
            rows = slice(6 * third, 6 * third + 6)
            for to, first, size in ((4, 0, 32), (0, 32, 4)) if n % 2 else ((0, 0, 36),):
                first = first + 40 * third
                turned[rows, 36 * n + to : 36 * n + to + size] = got[n, GRADS, 0:6, first : first + size]
    start = 72 * group + 36 * xl + 18 * core
    block = (lax.broadcasted_iota(jnp.int32, (18, 128), 0) + start) // 128
    for here in range(4):

        @pl.when(2 * xl + core == here)
        def _():
            first = (0, 18, 0, 14)[here]
            for col in range(BLOCKS):
                step = col - block
                step = jnp.where(step < 0, step + BLOCKS, step)
                lanes = slice(128 * col, 128 * col + 128)
                if here == 2:
                    straight = jnp.concatenate([direct[col, 32:36, :], direct[col, 0:14, :]], axis=0)
                else:
                    straight = direct[col, first : first + 18, :]
                value = jnp.where(step < HALF, straight, turned[:18, lanes]) / total
                for i in range(18):
                    out[i, :, lanes] = value[i : i + 1, :]


def factor_rows(got, direct, total, eig_a, eig_g):
    vmem = pl.BlockSpec(memory_space=pltpu.VMEM)
    out, scale = pl.pallas_call(
        rows_kernel,
        out_shape=(jax.ShapeDtypeStruct((18, 1, DA), F32), jax.ShapeDtypeStruct((DG, DA), F32)),
        in_specs=[vmem] * 5,
        out_specs=(vmem, vmem),
        scratch_shapes=[pltpu.VMEM((24, DA), F32)],
        compiler_params=pltpu.CompilerParams(vmem_limit_bytes=16 * 2**20),
        cost_estimate=pl.CostEstimate(flops=10**6, bytes_accessed=2**20, transcendentals=0),
        name="factor_rows",
    )(got, direct, total, eig_a, eig_g)
    return out.reshape(1, 18, DA), scale


def precond_kernel(got, other, total_ref, basis_a, basis_g, scale, g_factor, precond):
    core = lax.rem(lax.axis_index("dp"), 2)
    share = 1.0 / total_ref[0:1, 0:1]
    shape = (16, 2, GRADS + 1, 8, 128)
    both = (got[...].reshape(shape), other[...].reshape(shape))
    columns = []
    for col in range(WIDTH // 128):
        n, rest = divmod(col, 5)
        low, rest = (rest < 3), (rest if rest < 3 else rest - 3)
        tiles = jnp.where((core == 0) == low, both[0][:, n, rest], both[1][:, n, rest])
        columns.append(tiles.reshape(128, 128) * share)
    g_factor[0] = columns[-1]
    grad = jnp.concatenate([c.astype(BF16) for c in columns[:-1]], axis=1)
    left = lax.dot_general(basis_g[0], grad, (((0,), (0,)), ((), ())), preferred_element_type=F32).astype(BF16)
    rotated = jnp.dot(left, basis_a[0], preferred_element_type=F32)
    scaled = (rotated * scale[...]).astype(BF16)
    inner = jnp.dot(basis_g[0], scaled, preferred_element_type=F32).astype(BF16)
    precond[0] = lax.dot_general(inner, basis_a[0], (((1,), (1,)), ((), ())), preferred_element_type=F32)


def precondition(got, other, total, basis_a, basis_g, scale):
    vmem = pl.BlockSpec(memory_space=pltpu.VMEM)
    return pl.pallas_call(
        precond_kernel,
        out_shape=(jax.ShapeDtypeStruct((1, DG, DG), F32), jax.ShapeDtypeStruct((1, DG, DA), F32)),
        in_specs=[vmem] * 6,
        compiler_params=pltpu.CompilerParams(vmem_limit_bytes=16 * 2**20),
        name="precondition",
    )(got, other, total, basis_a, basis_g, scale)


def swap_cores(value):
    return lax.ppermute(value, "dp", [(i, i ^ 1) for i in range(64)])


def group_sum(value):
    for k in (1, 3):
        value = value + lax.ppermute(value, "grp", [(i, i ^ k) for i in range(4)])
    return value


def exchange(value, groups):
    return lax.all_to_all(value, "dp", 0, 0, axis_index_groups=groups, tiled=True)


def on_device(patches, out_grads, counts, basis_a, basis_g, eig_a, eig_g):
    mine, theirs = gram(patches, out_grads, counts)
    line = collect(exchange(mine + swap_cores(theirs), FIRST))
    done = group_sum(collect(exchange(line, SECOND)))
    send, direct, total = spread(done, swap_cores(done))
    got = exchange(send, CHIP_GROUPS)
    other = swap_cores(got)
    a_factor, scale = factor_rows(got, direct, total, eig_a, eig_g)
    g_factor, precond = precondition(got, other, total, basis_a, basis_g, scale)
    return a_factor, g_factor, precond


def solution(mesh):
    both = ("dp", "grp")
    placed = (P(None, both, None), P(None, both, None), P(both), P(), P(), P(), P())
    return jax.shard_map(
        on_device,
        mesh=mesh,
        in_specs=placed,
        out_specs=(P(None, "dp", None), P(), P()),
        check_vma=False,
    )
```
